32 devices in a mesh: seq: 4 (over y, x), batch: 8 (over z, core).
Axes of the slice: x: 2, y: 2, z: 4, core: 2. Of those that a mesh axis runs over, the one named last changes fastest.
Arguments:
- hidden_in: bfloat16 [8, 1536, 512], P('batch', 'seq'), may hold values from -6 to 6
- out_grad: bfloat16 [8, 1536, 512], P('batch', 'seq'), may hold values from -6 to 6
- start_flags: int32 [8, 1536], P('batch', 'seq'), may hold values 0 or 1
- ln_gain: bfloat16 [2, 2, 512], replicated, may hold values from 0.5 to 1.5
- ln_bias: bfloat16 [2, 2, 512], replicated, may hold values from -1.5 to 1.5
- w_qkv: bfloat16 [2, 512, 1536], replicated, may hold values from -0.25 to 0.25
- w_out: bfloat16 [2, 512, 512], replicated, may hold values from -0.75 to 0.75
- slopes: float32 [2, 8], replicated, may hold values from 0.00032552084 to 0.1
- w_in: bfloat16 [2, 512, 2048], replicated, may hold values from -0.25 to 0.25
- b_in: bfloat16 [2, 2048], replicated, may hold values from -1.5 to 1.5
- w_back: bfloat16 [2, 2048, 512], replicated, may hold values from -0.125 to 0.125
- b_back: bfloat16 [2, 512], replicated, may hold values from -1.5 to 1.5
- w_pool: bfloat16 [1536, 512], replicated, may hold values from -0.15625 to 0.15625
- b_pool: bfloat16 [512], replicated, may hold values from -1.5 to 1.5
- w_up: bfloat16 [512, 1536], replicated, may hold values from -0.25 to 0.25
- b_up: bfloat16 [1536], replicated, may hold values from -1.5 to 1.5
Outputs:
- block_out: bfloat16 [8, 1536, 512], P('batch', 'seq')
- hidden_grad: float32 [8, 1536, 512], P('batch', 'seq')
- ln_gain_grad: float32 [2, 2, 512], P(None, None, 'batch')
- ln_bias_grad: float32 [2, 2, 512], P(None, None, 'batch')
- w_qkv_grad: float32 [2, 512, 1536], P(None, None, 'batch')
- w_out_grad: float32 [2, 512, 512], P(None, None, 'batch')
- slopes_grad: float32 [2, 8], replicated
- w_in_grad: float32 [2, 512, 2048], P(None, None, 'batch')
- b_in_grad: float32 [2, 2048], P(None, 'batch')
- w_back_grad: float32 [2, 2048, 512], P(None, None, 'batch')
- b_back_grad: float32 [2, 512], P(None, 'batch')
- w_pool_grad: float32 [1536, 512], P(None, 'batch')
- b_pool_grad: float32 [512], P('batch')
- w_up_grad: float32 [512, 1536], P(None, 'batch')
- b_up_grad: float32 [1536], P('batch')
The draws below stay inside these ranges and needn't reach their ends.
All inputs are finite; a program needn't handle non-finite values. No bound on the sum of `start_flags` on one device may be relied on, other than what follows from the above.
Results may differ from the reference program's by a relative error of at most 0.028.
Values may be sent and summed in bfloat16 or wider, within the bound.
No kernel may reach another device: no remote copies, remote signals or barrier semaphores. Data moves between devices by JAX's collectives and lax.ppermute only.
A program may use at most 192 MiB of HBM per device.

```python
import math
import jax
import jax.numpy as jnp
from jax import lax

D = 512
HEADS = 8
HEAD = 64
FF = 2048
POOL_DEV = 128
ROWS_DEV = 384
LEN = 1536
SEQS = 8


def touch_ends(entries, rng, smallest, top_value):
    spot = [jax.random.randint(jax.random.fold_in(rng, axis), (), 0, length) for axis, length in enumerate(entries.shape)]
    widest = entries.shape.index(max(entries.shape))
    neighbour = spot[:widest] + [(spot[widest] + 1) % entries.shape[widest]] + spot[widest + 1:]
    return entries.at[tuple(spot)].set(smallest).at[tuple(neighbour)].set(top_value)


def block_levels(rng, shape, cuts, least, top_value):
    level, own = 1.0, jax.random.fold_in(rng, 6)
    for position, shards_of in cuts:
        heights = jnp.exp(jax.random.uniform(jax.random.fold_in(own, position), (shards_of,), jnp.float32, least / len(cuts), top_value / len(cuts)))
        level = level * jnp.repeat(heights, shape[position] // shards_of).reshape([-1 if axis == position else 1 for axis in range(len(shape))])
    return level


def noise(stream_key, shape, scale, most, shards=(), kind=jnp.bfloat16):
    gain = block_levels(stream_key, shape, shards, -0.22, 0.18) if shards else 1.0
    values = jax.random.normal(stream_key, shape, jnp.float32) * scale * gain
    return jnp.minimum(jnp.maximum(values, -most), most).astype(kind)


def setup_inputs(seed: int = 0) -> dict:
    streams_of = jax.random.split(jax.random.key(seed), 17)
    hidden_in = noise(streams_of[0], (SEQS, LEN, D), 1.0, 6.0, ((0, 8), (1, 4)))
    out_grad = noise(streams_of[1], (SEQS, LEN, D), 1.0, 6.0, ((0, 8), (1, 4)))
    start_flags = touch_ends((jax.random.randint(streams_of[2], (SEQS, LEN), 0, 4) < 3).astype(jnp.int32), jax.random.fold_in(streams_of[2], 1), 0, 1)
    ln_gain = jnp.clip(1.0 + 0.1 * jax.random.normal(streams_of[3], (2, 2, D), jnp.float32), 0.5, 1.5).astype(jnp.bfloat16)
    ln_bias = noise(streams_of[4], (2, 2, D), 0.3, 1.5)
    w_qkv = noise(streams_of[5], (2, D, 3 * D), D ** -0.5, 0.25)
    w_out = noise(streams_of[6], (2, D, D), (D // 8) ** -0.5, 0.75)
    slopes = jnp.clip(jnp.exp(jax.random.uniform(streams_of[7], (2, HEADS), jnp.float32, math.log(0.00032552084), math.log(0.1))), 0.00032552084, 0.1)
    w_in = noise(streams_of[8], (2, D, FF), D ** -0.5, 0.25)
    b_in = noise(streams_of[9], (2, FF), 0.3, 1.5)
    w_back = noise(streams_of[10], (2, FF, D), FF ** -0.5, 0.125)
    b_back = noise(streams_of[11], (2, D), 0.3, 1.5)
    w_pool = noise(streams_of[12], (3 * D, D), (3 * D) ** -0.5, 0.15625)
    b_pool = noise(streams_of[13], (D,), 0.3, 1.5)
    w_up = noise(streams_of[14], (D, 3 * D), D ** -0.5, 0.25)
    b_up = noise(streams_of[15], (3 * D,), 0.3, 1.5)
    return {"hidden_in": hidden_in, "out_grad": out_grad, "start_flags": start_flags, "ln_gain": ln_gain, "ln_bias": ln_bias, "w_qkv": w_qkv, "w_out": w_out, "slopes": slopes, "w_in": w_in, "b_in": b_in, "w_back": w_back, "b_back": b_back, "w_pool": w_pool, "b_pool": b_pool, "w_up": w_up, "b_up": b_up}


EPSILON = 1e-05
NEGATIVE = -1e+30

@jax.custom_vjp
def low(v):
    return lax.optimization_barrier(v.astype(jnp.bfloat16)).astype(jnp.float32)

@jax.custom_vjp
def low_back(v):
    return v

def low_keep(v):
    return (low(v), None)

def low_pass(kept, grad):
    return (grad,)

def back_keep(v):
    return (v, None)

def back_low(kept, grad):
    return (low(grad),)
low.defvjp(low_keep, low_pass)
low_back.defvjp(back_keep, back_low)

def product(left, right):
    return jnp.dot(left, right, precision=lax.Precision.HIGHEST, preferred_element_type=jnp.float32)

def normalize(values_in, gain_row, bias_row):
    row_mean = lax.optimization_barrier(jnp.mean(values_in, axis=-1, keepdims=True))
    centred = values_in - row_mean
    spread = lax.optimization_barrier(jnp.mean(centred * centred, axis=-1, keepdims=True))
    return centred * lax.rsqrt(spread + EPSILON) * gain_row + bias_row

def attend(queries, keys_in, values_in, slope_row, block_rows):
    length = queries.shape[0]
    count = length // block_rows
    query_blocks = queries.reshape(count, block_rows, HEADS, HEAD)
    key_heads = keys_in.reshape(length, HEADS, HEAD)
    value_heads = values_in.reshape(length, HEADS, HEAD)
    starts = jnp.arange(count, dtype=jnp.int32) * block_rows

    def one_block(block_item):
        query_block, block_start = block_item
        raw_scores = jnp.einsum('qhe,khe->hqk', query_block, key_heads, precision=lax.Precision.HIGHEST) * HEAD ** (-0.5)
        distance = (block_start + jnp.arange(block_rows, dtype=jnp.int32)[:, None] - jnp.arange(length, dtype=jnp.int32)[None, :]).astype(jnp.float32)
        scores = low_back(raw_scores - slope_row[:, None, None] * distance[None])
        scores = jnp.where(distance[None] >= 0, scores, NEGATIVE)
        soft_weights = low(jax.nn.softmax(scores, axis=-1))
        mixed = jnp.einsum('hqk,khe->qhe', soft_weights, value_heads, precision=lax.Precision.HIGHEST)
        return mixed.reshape(block_rows, HEADS * HEAD)
    mixed = lax.map(jax.checkpoint(one_block), (query_blocks, starts))
    return mixed.reshape(length, HEADS * HEAD)

def layer(values_in, weights, which, block_rows):
    ln_gain, ln_bias, w_qkv, w_out, slopes, w_in, b_in, w_back, b_back = weights
    attn_in = low(normalize(values_in, ln_gain[which, 0], ln_bias[which, 0]))
    qkv_rows = low_back(low(product(attn_in, w_qkv[which])))
    mixed = low_back(low(attend(qkv_rows[:, :D], qkv_rows[:, D:2 * D], qkv_rows[:, 2 * D:], slopes[which], block_rows)))
    middle = values_in + low_back(product(mixed, w_out[which]))
    ffn_in = low(normalize(middle, ln_gain[which, 1], ln_bias[which, 1]))
    pre_act = low_back(product(ffn_in, w_in[which]) + b_in[which])
    activated = low(jax.nn.gelu(pre_act))
    return middle + low_back(product(activated, w_back[which]) + b_back[which])

def forward(values_in, ln_gain, ln_bias, w_qkv, w_out, slopes, w_in, b_in, w_back, b_back, w_pool, b_pool, w_up, b_up):
    weights = (ln_gain, ln_bias, w_qkv, w_out, slopes, w_in, b_in, w_back, b_back)
    full_out = layer(values_in, weights, 0, ROWS_DEV)
    kept = low(full_out)
    shifted = jnp.concatenate([jnp.zeros((2, D), jnp.float32), kept[:-2]], axis=0)
    grouped = shifted.reshape(LEN // 3, 3 * D)
    pooled = low_back(product(grouped, w_pool) + b_pool)
    short_out = layer(pooled, weights, 1, POOL_DEV)
    up_rows = low_back(product(low(short_out), w_up) + b_up)
    return full_out + up_rows.reshape(LEN, D)

def reference(hidden_in, out_grad, start_flags, ln_gain, ln_bias, w_qkv, w_out, slopes, w_in, b_in, w_back, b_back, w_pool, b_pool, w_up, b_up):
    params = tuple((param.astype(jnp.float32) for param in (ln_gain, ln_bias, w_qkv, w_out, slopes, w_in, b_in, w_back, b_back, w_pool, b_pool, w_up, b_up)))

    def one_sequence(totals, block_item):
        values_in, cotangent, flag_row = block_item
        output, pull = jax.vjp(forward, values_in.astype(jnp.float32), *params)
        grads = pull(cotangent.astype(jnp.float32) * flag_row.astype(jnp.float32)[:, None])
        new_totals = tuple((total + grad for total, grad in zip(totals, grads[1:])))
        return (new_totals, (output.astype(jnp.bfloat16), grads[0]))
    start_totals = tuple((jnp.zeros(param.shape, jnp.float32) for param in params))
    totals, (outputs, input_grads) = lax.scan(one_sequence, start_totals, (hidden_in, out_grad, start_flags))
    return (outputs, input_grads, totals[0], totals[1], totals[2], totals[3], totals[4], totals[5], totals[6], totals[7], totals[8], totals[9], totals[10], totals[11], totals[12])
```

```python
import jax
import jax.numpy as jnp
from jax import lax
from jax.experimental import pallas as pl
from jax.experimental.pallas import tpu as pltpu
from jax.sharding import PartitionSpec as P

EPSILON = 1e-05
NEGATIVE = -1e30
HEAD = 64
SCALE = HEAD ** (-0.5)
POS = 128
BQ = 256
F32 = jnp.float32
BF = jnp.bfloat16
VMEM_LIMIT = 60 * 1024 * 1024
GELU_A = 0.7978845608028654
GELU_B = 0.044715


def dims(a, b, ca, cb):
    return lax.dot_general(a, b, (((ca,), (cb,)), ((), ())), preferred_element_type=F32)


def mm(a, b):
    return dims(a, b, 1, 0)


def nt(a, b):
    return dims(a, b, 1, 1)


def tn(a, b):
    return dims(a, b, 0, 0)


def flip(a):
    return jnp.transpose(a)


def iota(shape, axis):
    return lax.broadcasted_iota(jnp.int32, shape, axis)


def standard(x):
    centred = x - jnp.mean(x, axis=-1, keepdims=True)
    rstd = lax.rsqrt(jnp.mean(centred * centred, axis=-1, keepdims=True) + EPSILON)
    return centred * rstd, rstd


TILE = 64


def tiles(rows, size):
    return [slice(at, min(at + size, rows)) for at in range(0, rows, size)]


def norm_into(source, gain, bias, target, first=0):
    rows = source.rows
    for tile in tiles(rows, TILE):
        target[pl.ds(first + tile.start, tile.stop - tile.start), :] = (
            standard(source(tile))[0] * gain + bias
        ).astype(BF)


class Rows:
    def __init__(self, rows, read):
        self.rows, self.read = rows, read

    def __call__(self, tile):
        return self.read(tile)


def norm_back(x, gain, grad, put, rows):
    gain_sum = bias_sum = None
    for tile in tiles(rows, TILE):
        xhat, rstd = standard(x(tile))
        given = grad(tile)
        inner = given * gain
        put(
            tile,
            rstd
            * (
                inner
                - jnp.mean(inner, axis=-1, keepdims=True)
                - xhat * jnp.mean(inner * xhat, axis=-1, keepdims=True)
            ),
        )
        one = jnp.sum(given * xhat, axis=0, keepdims=True)
        two = jnp.sum(given, axis=0, keepdims=True)
        gain_sum = one if gain_sum is None else gain_sum + one
        bias_sum = two if bias_sum is None else bias_sum + two
    return gain_sum, bias_sum


def ffn_forward(normal, w_in, b_in, act, rate, rows, ff):
    for lanes in tiles(ff, 256):
        for tile in tiles(rows, 128):
            value, slope = gelu_both(mm(normal[tile, :], w_in[:, lanes]) + b_in[0:1, lanes])
            act[tile, lanes] = value.astype(BF)
            rate[tile, lanes] = slope.astype(BF)


def ffn_backward(branch, w_back, rate, dpre, sums, rows, ff):
    for lanes in tiles(ff, 512):
        value = (nt(branch[...], w_back[lanes, :]) * rate[:, lanes].astype(F32)).astype(BF)
        dpre[:, lanes] = value
        sums[:, lanes] = jnp.sum(value.astype(F32), axis=0, keepdims=True)


def gelu_both(x):
    square = x * x
    half = 0.5 * jnp.tanh(x * (GELU_A + GELU_A * GELU_B * square)) + 0.5
    value = x * half
    return value, half + (value - value * half) * (2.0 * GELU_A + 6.0 * GELU_A * GELU_B * square)


def rows_at(start, size):
    return pl.ds(pl.multiple_of(start, 16), size)


def lone(value, lane):
    return jnp.where(iota((1, 128), 1) == lane, value, 0.0)


def spread(target, first, value):
    for l in range(target.shape[0]):
        target[l, pl.ds(first, value.shape[0], stride=3), :] = value[:, l * 128 : (l + 1) * 128]


def lanes_at(ref, start, width):
    if width % 128 == 0:
        return ref[:, pl.ds(pl.multiple_of(start, 128), width)]
    total = ref.shape[1]
    pick = (iota((total, width), 0) == iota((total, width), 1) + start).astype(F32).astype(BF)
    return mm(ref[...], pick).astype(BF)


def place_positions(kaug, width):
    length = kaug.shape[0]
    row = iota((length, POS), 0)
    lane = iota((length, POS), 1)
    value = jnp.where(lane < 3, (row >> 7) << 7, jnp.where(lane < 6, row & 127, 0))
    kaug[:, width : width + POS] = value.astype(F32).astype(BF)


def slope_rows(slope, length):
    full = jnp.full((POS, length), slope, F32)
    first = full.astype(BF)
    rest = full - first.astype(F32)
    second = rest.astype(BF)
    third = (rest - second.astype(F32)).astype(BF)
    row = iota((POS, length), 0)
    part = jnp.where(
        (row == 0) | (row == 3),
        first.astype(F32),
        jnp.where(
            (row == 1) | (row == 4),
            second.astype(F32),
            jnp.where((row == 2) | (row == 5), third.astype(F32), 0.0),
        ),
    )
    return part.astype(BF)


def prepare(q, k, slopes, kaug, qa):
    length, width = q.shape
    kaug[:, 0:width] = k
    turned = flip(q) * SCALE
    row = iota((width, length), 0)
    for h, slope in enumerate(slopes):
        own = (row >= HEAD * h) & (row < HEAD * h + HEAD)
        qa[h, 0:width, :] = jnp.where(own, turned, 0.0).astype(BF)
        qa[h, width : width + POS, :] = slope_rows(slope, length)


def causal():
    return iota((BQ, BQ), 0) <= iota((BQ, BQ), 1)


def attend(kaug, qa, vt, mixt, lse, heads):
    length = kaug.shape[0]
    for i in range(length // BQ):
        here = slice(i * BQ, (i + 1) * BQ)
        spans = [slice(j * BQ, (j + 1) * BQ) for j in range(i + 1)]
        for h in range(heads):
            qh = qa[h, :, here]
            scores, top = [], None
            for span in spans:
                score = mm(kaug[span, :], qh)
                if span == here:
                    score = jnp.where(causal(), score, NEGATIVE)
                scores.append(score)
                one = jnp.max(score, axis=0, keepdims=True)
                top = one if top is None else jnp.maximum(top, one)
            own = slice(HEAD * h, HEAD * h + HEAD)
            total = out = None
            for span, score in zip(spans, scores):
                soft = jnp.exp(score - top)
                one = jnp.sum(soft, axis=0, keepdims=True)
                part = mm(vt[own, span], soft.astype(BF))
                total = one if total is None else total + one
                out = part if out is None else out + part
            mixt[own, here] = out / total
            lse[h : h + 1, here] = top + jnp.log(total)


def attend_back(kaug, qa, v, kta, qm, doa, dom, delta, lse, dk, dv, dqt, heads):
    length = kaug.shape[0]
    dk[...] = jnp.zeros_like(dk)
    dv[...] = jnp.zeros_like(dv)
    slope_sums = [jnp.zeros((1, BQ), F32) for _ in range(heads)]
    for i in range(length // BQ):
        off = i * BQ
        here = slice(off, off + BQ)
        for h in range(heads):
            qh = qa[h, :, here]
            doh = doa[h, :, here]
            row_lse = lse[h : h + 1, here]
            row_delta = delta[h : h + 1, here]
            queries = qm[h, here, :]
            grads = dom[h, here, :]
            turned = None
            for part in ((here, True),) + (((slice(0, off), False),) if off else ()):
                span, masked = part
                soft = jnp.exp(mm(kaug[span, :], qh) - row_lse)
                if masked:
                    soft = jnp.where(causal(), soft, 0.0)
                score = (soft * (mm(v[span, :], doh) - row_delta)).astype(BF)
                dv[span, :] += mm(soft.astype(BF), grads)
                dk[span, :] += mm(score, queries)
                more = mm(kta[h, :, span], score)
                turned = more if turned is None else turned + more
            dqt[HEAD * h : HEAD * h + HEAD, here] = turned[0:HEAD, :] * SCALE
            spot = (off + iota((1, BQ), 1)).astype(F32)
            slope_sums[h] = slope_sums[h] + (
                turned[HEAD + 1 : HEAD + 2, :]
                + turned[HEAD + 2 : HEAD + 3, :]
                - spot * turned[HEAD : HEAD + 1, :]
            )
    return slope_sums


def prepare_back(q, k, do, mixt, kta, qm, doa, dom, delta, heads):
    length, width = q.shape
    kt = flip(k)
    dot = flip(do)
    lane = iota((length, width), 1)
    row = iota((width, length), 0)
    extra = iota((16, length), 0)
    column = iota((16, length), 1)
    extras = jnp.where(
        extra == 0,
        1,
        jnp.where(extra == 1, (column >> 7) << 7, jnp.where(extra == 2, column & 127, 0)),
    )
    for h in range(heads):
        own = slice(HEAD * h, HEAD * h + HEAD)
        kta[h, 0:HEAD, :] = kt[own, :].astype(BF)
        kta[h, HEAD : HEAD + 16, :] = extras.astype(F32).astype(BF)
        mine = (lane >= HEAD * h) & (lane < HEAD * h + HEAD)
        qm[h] = jnp.where(mine, q.astype(F32) * SCALE, 0.0).astype(BF)
        dom[h] = jnp.where(mine, do.astype(F32), 0.0).astype(BF)
        doa[h] = jnp.where((row >= HEAD * h) & (row < HEAD * h + HEAD), dot, 0.0).astype(BF)
        delta[h : h + 1, :] = jnp.sum(dot[own, :] * mixt[own, :], axis=0, keepdims=True)


def attend_scratch(length, width, heads, lead=()):
    wide = width + POS
    return [
        pltpu.VMEM(lead + (length, wide), BF),
        pltpu.VMEM(lead + (heads, wide, length), BF),
    ]


def back_scratch(length, width, heads):
    return [
        pltpu.VMEM((heads, HEAD + 16, length), BF),
        pltpu.VMEM((heads, length, width), BF),
        pltpu.VMEM((heads, width, length), BF),
        pltpu.VMEM((heads, length, width), BF),
        pltpu.VMEM((8, length), F32),
        pltpu.VMEM((length, width), F32),
        pltpu.VMEM((length, width), F32),
        pltpu.VMEM((width, length), F32),
    ]


NEAR = "near"
HELD = "held"
ALL = -1
LOAD = -2
FAR = "far"
PART = "part"
HOLD = "hold"
RAW = "raw"


def keeps(n):
    return n <= 4


def hold(n):
    return HOLD if keeps(n) else FAR


def held(n):
    return HELD if keeps(n) else ALL


def smem():
    return pl.BlockSpec(memory_space=pltpu.SMEM)


def vmem():
    return pl.BlockSpec(memory_space=pltpu.VMEM)


def anywhere():
    return pl.BlockSpec(memory_space=pl.ANY)


class Held:
    def __init__(self, source, target, semaphore):
        self.copy = pltpu.make_async_copy(source, target, semaphore)
        self.target = target
        self.waited = False
        self.copy.start()

    def get(self):
        if not self.waited:
            self.copy.wait()
            self.waited = True
        return self.target


class Far:
    def __init__(self, ref, out, semaphores):
        self.ref, self.out, self.semaphores = ref, out, semaphores
        self.copies = []

    def send(self, index=None):
        source = self.ref if index is None else self.ref.at[index]
        target = self.out if index is None else self.out.at[index]
        self.copies.append(pltpu.make_async_copy(source, target, self.semaphores.at[len(self.copies)]))
        self.copies[-1].start()

    def finish(self):
        if not self.copies:
            self.send()
        for copy in self.copies:
            copy.wait()


class Here:
    def __init__(self, ref):
        self.ref = ref

    def get(self):
        return self.ref

    def send(self, index=None):
        pass

    def finish(self):
        pass


def padded(shape, dtype):
    lead = 1
    for extent in shape[:-2]:
        lead *= extent
    tall = shape[-2] if len(shape) > 1 else 1
    return lead * -(-tall // 16) * 16 * -(-shape[-1] // 128) * 128 * jnp.dtype(dtype).itemsize


def in_hbm(array):
    return pltpu.with_memory_space_constraint(array, pltpu.HBM)


def in_vmem(array):
    return pltpu.with_memory_space_constraint(array, pltpu.VMEM)


def call(body, name, ins, specs, outs, scratch=(), after=(), spare=10, weight=10, aliases=None):
    held = [i for i, spec in enumerate(specs) if isinstance(spec, int)]
    shapes = [ins[i].shape[1:] if specs[i] >= 0 else ins[i].shape for i in held]
    kinds = [out[2] if len(out) > 2 else NEAR for out in outs]
    far = [i for i, kind in enumerate(kinds) if kind in (FAR, PART)]
    far_shapes = [out[0] if kind is FAR else out[0][1:] for out, kind in zip(outs, kinds)]
    more = [pltpu.VMEM(shape, ins[i].dtype) for i, shape in zip(held, shapes)]
    more += [pltpu.VMEM(far_shapes[i], outs[i][1]) for i in far]
    if held:
        more.append(pltpu.SemaphoreType.DMA((len(held),)))
    if far:
        more.append(pltpu.SemaphoreType.DMA((len(far), 8)))
    count, own = len(ins), len(scratch)
    used = sum(padded(shape, ins[i].dtype) for i, shape in zip(held, shapes))
    used += sum(padded(shape, out[1]) for shape, out, kind in zip(far_shapes, outs, kinds) if kind is not HOLD)
    used += sum(padded(a.shape, a.dtype) for a, spec in zip(ins, specs) if spec is NEAR)
    used += sum(padded(s.shape, s.dtype) for s in scratch if len(s.shape) > 1 and s.dtype in (F32, BF))
    limit = min(VMEM_LIMIT, int(used * (1.1 if spare >= 10 else 1.0)) + spare * 1024 * 1024)

    def kernel(*refs):
        refs = list(refs)
        operands = refs[:count]
        results = refs[count + len(after) : count + len(after) + len(outs)]
        rest = refs[count + len(after) + len(outs) :]
        temporary, rest = rest[:own], rest[own:]
        targets, rest = rest[: len(held)], rest[len(held) :]
        sources, rest = rest[: len(far)], rest[len(far) :]
        for at, i in enumerate(held):
            source = operands[i] if specs[i] < 0 else operands[i].at[specs[i]]
            operands[i] = Held(source, targets[at], rest[0].at[at])
        for at, i in enumerate(far):
            target = results[i].at[outs[i][3]] if kinds[i] is PART else results[i]
            results[i] = Far(sources[at], target, rest[-1].at[at])
        for i, kind in enumerate(kinds):
            results[i] = Here(results[i]) if kind is HOLD else results[i]
        for i, spec in enumerate(specs):
            operands[i] = Here(operands[i]) if spec is HELD else operands[i]
        body(*operands, *results, *temporary)
        for i in held:
            operands[i].get()
        for i in far:
            results[i].finish()

    pinned = pl.BlockSpec(memory_space=pltpu.HBM)
    spec_of = lambda spec: anywhere() if spec == LOAD else pinned if isinstance(spec, int) or spec is RAW else vmem() if spec in (NEAR, HELD) else spec
    shape_of = {NEAR: jax.ShapeDtypeStruct, HOLD: pltpu.VMEM, FAR: pltpu.HBM, PART: pltpu.HBM}
    place = lambda a, spec: in_hbm(a) if spec is RAW or isinstance(spec, int) and spec != LOAD else in_vmem(a) if spec is HELD else a
    return pl.pallas_call(
        kernel,
        out_shape=[shape_of[kind](out[0], out[1]) for out, kind in zip(outs, kinds)],
        in_specs=[spec_of(spec) for spec in specs] + [anywhere()] * len(after),
        out_specs=[pinned if kind in (FAR, PART) else vmem() for kind in kinds],
        scratch_shapes=list(scratch) + more,
        compiler_params=pltpu.CompilerParams(vmem_limit_bytes=limit),
        cost_estimate=pl.CostEstimate(flops=weight * 1000000000, bytes_accessed=0, transcendentals=0),
        name=name,
        input_output_aliases=aliases or {},
    )(*[place(a, spec) for a, spec in zip(ins, specs)], *after)


def fold(name, targets, after=(), kind=NEAR, weight=10):
    arrays = []
    for _, blocks in targets:
        for block in blocks:
            for array, _, _ in block:
                if not any(array is other for other in arrays):
                    arrays.append(array)
    where = lambda array: [i for i, other in enumerate(arrays) if other is array][0]
    outs, plan = [], []
    for dtype, blocks in targets:
        outs.append(((sum(block[0][2] for block in blocks), blocks[0][0][0].shape[-1]), dtype) + ((kind,) if kind is HOLD else ()))
        plan.append([(block[0][2], [(where(a), first) for a, first, _ in block]) for block in blocks])

    def body(*refs):
        for target, blocks in zip(refs[len(arrays) :], plan):
            target = target.ref if isinstance(target, Here) else target
            at = 0
            for count, block in blocks:
                total = sum(refs[i][first : first + count, :].astype(F32) for i, first in block)
                target[at : at + count, :] = total.astype(target.dtype)
                at += count

    return call(body, name, arrays, [NEAR] * len(arrays), outs, after=after, weight=weight)


def mask_rows(out_grad, flags, after):
    rows, d = out_grad.shape
    third = rows // 3

    def body(grad_ref, flag_ref, given, whole):
        kept = jnp.where(flag_ref[...] != 0, grad_ref[...].astype(F32), 0.0)
        for l in range(d // 128):
            whole[l] = kept[:, l * 128 : (l + 1) * 128]
        for c in range(3):
            for l in range(d // 128):
                part = slice(c * d + l * 128, c * d + (l + 1) * 128)
                given[:, part] = whole[l, pl.ds(c, third, stride=3), :].astype(BF)

    return call(
        body,
        "mask_rows",
        [out_grad, flags],
        [NEAR, NEAR],
        [((third, 3 * d), BF)],
        [pltpu.VMEM((d // 128, rows, 128), F32)],
        after=after,
    )[0]


def pass_on(array, after, weight=10):
    def body(source, target):
        target[...] = source[...]

    return call(body, "pass_on", [array], [NEAR], [(array.shape, array.dtype)], after=after, weight=weight)[0]


def first_rows(pieces, wq, lnp):
    rows, d = pieces[0].shape
    width = wq.shape[1]

    def body(*refs):
        piece_refs, (w_ref, ln_ref, attn, qkv) = refs[: len(pieces)], refs[len(pieces) :]
        for k in range(len(pieces)):
            here = slice(k * rows, (k + 1) * rows)
            norm_into(
                Rows(rows, lambda tile, k=k: piece_refs[k][tile, :].astype(F32)),
                ln_ref[0:1, :],
                ln_ref[4:5, :],
                attn,
                k * rows,
            )
            qkv[here, :] = mm(attn[here, :], w_ref.get()[...]).astype(BF)

    outs = [((len(pieces) * rows, d), BF), ((len(pieces) * rows, width), BF)]
    return call(body, "first_rows", [*pieces, wq, lnp], [NEAR] * len(pieces) + [ALL, NEAR], outs)


def first_attention(idx, slopes, pieces, early, wq, lnp, weights, head_count, dh, after):
    n = len(pieces)
    given = [k for k in range(n) if pieces[k] is not None]
    gone = [k for k in range(n) if pieces[k] is None]
    rows, d = pieces[given[0]].shape
    width = wq.shape[1] // 3
    length = n * rows

    def body(*refs):
        idx_ref, slope_ref = refs[0], refs[1]
        piece_refs = dict(zip(given, refs[2 : 2 + len(given)]))
        early_attn, early_qkv, w_ref, ln_ref = refs[2 + len(given) : 6 + len(given)]
        refs = refs[6 + len(given) :]
        sources, refs = refs[: len(weights)], refs[len(weights) :]
        sends, refs = refs[:n], refs[n:]
        attn, qkv, mixt, lse = refs[:4]
        targets, refs = refs[4 : 4 + len(weights)], refs[4 + len(weights) :]
        kaug, qa, vt, whole = refs[:4]
        s = idx_ref[0]
        loads = [
            pltpu.make_async_copy(source if layer is None else source.at[layer], target.ref, refs[4].at[i])
            for i, (source, target, (_, layer)) in enumerate(zip(sources, targets, weights))
        ]
        for load in loads:
            load.start()
        place_positions(kaug, width)
        gain, bias = ln_ref[0:1, :], ln_ref[4:5, :]
        own_weights = None
        for i, k in enumerate(gone):
            at, here = rows_at((s ^ k) * rows, rows), slice(i * rows, (i + 1) * rows)
            attn.ref[at, :] = early_attn[here, :]
            qkv.ref[at, :] = early_qkv[here, :]
        for k in given:
            first = pl.multiple_of((s ^ k) * rows, TILE)
            norm_into(
                Rows(rows, lambda tile, k=k: piece_refs[k][tile, :].astype(F32)), gain, bias, attn.ref, first
            )
            if own_weights is None:
                own_weights = w_ref.get()
            at = rows_at((s ^ k) * rows, rows)
            qkv.ref[at, :] = mm(attn.ref[at, :], own_weights[...]).astype(BF)
        attn.send()
        qkv.send()
        prepare(
            qkv.ref[:, 0:width],
            qkv.ref[:, width : 2 * width],
            [slope_ref[0, s * head_count + h] for h in range(head_count)],
            kaug,
            qa,
        )
        vt[...] = flip(qkv.ref[:, 2 * width :]).astype(BF)
        if dh < width:
            mixt.ref[...] = jnp.zeros(mixt.ref.shape, F32)
        attend(kaug, qa, vt, mixt.ref, lse.ref, head_count)
        mixt.send()
        lse.send()
        whole[...] = flip(mixt.ref[...].astype(BF))
        for k in range(n):
            sends[k][...] = whole[rows_at((s ^ k) * rows, rows), 0:dh]
        for load in loads:
            load.wait()

    outs = [((rows, dh), BF)] * n + [
        ((length, d), BF, hold(n)),
        ((length, 3 * width), BF, hold(n)),
        ((width, length), F32, hold(n)),
        ((8, length), F32, hold(n)),
    ]
    outs += [(weight.shape[-2:], BF, HOLD) for weight, _ in weights]
    scratch = attend_scratch(length, width, head_count) + [
        pltpu.VMEM((width, length), BF),
        pltpu.VMEM((length, width), BF),
        pltpu.SemaphoreType.DMA((max(len(weights), 1),)),
    ]
    result = call(
        body,
        "first_attention",
        [idx, slopes, *[pieces[k] for k in given], *early, wq, lnp, *[in_hbm(weight) for weight, _ in weights]],
        [smem(), smem()] + [NEAR] * (len(given) + 2) + [ALL, NEAR] + [pl.BlockSpec(memory_space=pltpu.HBM)] * len(weights),
        outs,
        scratch,
        after=after,
    )
    return result[:n], result[n : n + 4], result[n + 4 :]


CARRY = 16


def first_ffn(idx, hid, mixes, lnp, w_out, w_in, b_in, w_back, b_back, w_pool, b_pool, after):
    n = len(mixes)
    rows, d = hid.shape
    dh = mixes[0].shape[1]
    ff = b_in.shape[1]
    third = rows // 3

    def body(*refs):
        idx_ref, hid_ref = refs[0], refs[1]
        mix_refs = refs[2 : 2 + n]
        ln_ref, wo, wi, bi, wb, bb, wp, bp = refs[2 + n : 10 + n]
        full_g, pooled, mid, pack, slope, whole, owners = refs[10 + n :]
        s = idx_ref[0]
        middle = hid_ref.get()[...].astype(F32)
        wo = wo.get()
        for k in range(n):
            middle = middle + mm(mix_refs[k][...], wo[rows_at((s ^ k) * dh, dh), :])
            owners[s ^ k] = mix_refs[k][...]
        for j in range(n):
            pack.ref[0:rows, ff + d + j * dh : ff + d + (j + 1) * dh] = owners[j]
        mid.ref[...] = middle
        mid.send()
        norm_into(
            Rows(rows, lambda tile: mid.ref[tile, :]), ln_ref[1:2, :], ln_ref[5:6, :], pack.ref.at[:, ff : ff + d]
        )
        wi, wb = wi.get(), wb.get()
        ffn_forward(pack.ref.at[:, ff : ff + d], wi, bi, pack.ref, slope.ref, rows, ff)
        slope.send()
        total = mid.ref[...] + bb[0:1, :] + mm(pack.ref[0:rows, 0:ff], wb[...])
        for l in range(d // 128):
            whole[l] = total[:, l * 128 : (l + 1) * 128]
        for c in range(3):
            for l in range(d // 128):
                some = whole[l, pl.ds(c, third, stride=3), :]
                part = slice(c * d + l * 128, c * d + (l + 1) * 128)
                full_g.ref[:, part] = some
                pack.ref[rows:, part] = some.astype(BF)
        pack.send()
        wp = wp.get()
        moved = pltpu.roll(mm(pack.ref[rows:, d : 3 * d], wp[0 : 2 * d, :]), 1, 0)
        own = mm(pack.ref[rows:, 0:d], wp[2 * d :, :]) + bp[0:1, :]
        pooled[0:third, :] = (own + jnp.where(iota((third, d), 0) == 0, 0.0, moved)).astype(BF)
        pooled[third:, :] = moved[0:CARRY, :].astype(BF)

    outs = [
        ((third, 3 * d), F32, hold(n)),
        ((third + CARRY, d), BF),
        ((rows, d), F32, hold(n)),
        ((rows + third, ff + 2 * d), BF, hold(n)),
        ((rows, ff), BF, hold(n)),
    ]
    weight = HELD if keeps(n) else 0
    return call(
        body,
        "first_ffn",
        [idx, hid, *mixes, lnp, w_out, w_in, b_in, w_back, b_back, w_pool, b_pool],
        [smem(), ALL] + [NEAR] * (n + 1) + [weight, weight, NEAR, weight, NEAR, ALL, NEAR],
        outs,
        [pltpu.VMEM((d // 128, rows, 128), F32), pltpu.VMEM((n, rows, dh), BF)],
        after=after,
    )


def short_layout(n, m, d, ff):
    kw = d // n
    spans, at = {}, 0
    for name, rows, blocks in (
        ("qkv", 3 * d // m, 1),
        ("out", d // m, 1),
        ("in", kw, ff // m // kw),
        ("back", d // m, ff // n // kw),
        ("up", 3 * d // m, 1),
    ):
        spans[name] = (at, rows, blocks)
        at += rows * blocks
    return spans, at


def ffn_layout(n, m, d, ff):
    kw = d // n
    spans, at = {}, 0
    for name, rows, blocks in (
        ("out", d // m, 1),
        ("in", kw, ff // m // kw),
        ("back", d // m, ff // n // kw),
    ):
        spans[name] = (at, rows, blocks)
        at += rows * blocks
    return spans, at


def last_layout(n, m, d):
    return 3 * d // m, d // m, 3


def pool_unit(unit, n, d):
    kw = d // n
    early = unit < 2 * n
    return early, jnp.where(early, d + unit * kw, unit * kw - 2 * d)


def short_start(idx, given, w_up, w_back, layered, w_pool, after):
    n = len(given)
    third, d3 = given[0].shape
    d, ff = d3 // 3, w_back.shape[0]
    length = n * third

    def body(*refs):
        idx_ref, given_refs = refs[0], refs[1 : 1 + n]
        wu, wb = refs[1 + n].get(), refs[2 + n].get()
        sources, refs = refs[3 + n : 7 + n], refs[7 + n :]
        u, grad, branch, act_grad = refs[:4]
        targets, arrived = refs[4:8], refs[8]
        s = idx_ref[0]
        loads = []
        later = [
            pltpu.make_async_copy(source.at[1] if i < 3 else source, target.ref, arrived.at[n + i])
            for i, (source, target) in enumerate(zip(sources, targets))
        ]
        for k in range(n):
            place = u.ref.at[rows_at((s ^ k) * third, third), :]
            loads.append(pltpu.make_async_copy(given_refs[k], place, arrived.at[k]))
        for load in loads:
            load.start()
        for load in later:
            load.start()
        for load in loads:
            load.wait()
        grad.ref[...] = nt(u.ref[...], wu[...])
        branch.ref[...] = grad.ref[...].astype(BF)
        for lanes in tiles(ff, 512):
            act_grad.ref[:, lanes] = nt(branch.ref[...], wb[lanes, :]).astype(BF)
        for load in later:
            load.wait()

    outs = [
        ((length, d3), BF, HOLD),
        ((length, d), F32, HOLD),
        ((length, d), BF, HOLD),
        ((length, ff), BF, HOLD),
        *[(weight.shape[1:], BF, HOLD) for weight in layered],
        (w_pool.shape, BF, HOLD),
    ]
    return call(
        body,
        "short_start",
        [idx, *given, w_up, w_back, *layered, w_pool],
        [smem()] + [anywhere()] * n + [HELD, HELD] + [RAW] * 4,
        outs,
        [pltpu.SemaphoreType.DMA((n + 4,))],
        after=after,
        weight=100,
    )


def short_layer(
    idx, slopes, pooled, given, begun, full_g, lnp, w_qkv, w_out, w_in, b_in, w_back, b_back, w_pool, w_up, b_up, m, after
):
    n = len(pooled)
    third = pooled[0].shape[0] - CARRY
    given = [] if begun else given
    d = lnp.shape[1]
    ff = b_in.shape[1]
    rows = 3 * third
    length = n * third
    width = 128
    pairs = d // width
    kw = d // n
    spans, packed_rows = short_layout(n, m, d, ff)
    kept_pairs = pairs if length <= 512 else 1

    def body(*refs):
        idx_ref, slope_ref = refs[0], refs[1]
        pool_refs = refs[2 : 2 + n]
        given_refs, refs = refs[2 + n : 2 + n + len(given)], refs[2 + n + len(given) :]
        begun_refs, refs = refs[: len(begun)], refs[len(begun) :]
        (fg, ln_ref, wq, wo, wi, bi, wb, bb, wp, wu, bu) = refs[:11]
        block_out, full_grad, pair, keep, give, small = refs[11:17]
        (
            pooled_s, carry, attn, qkv, mixed, mixt, lse, kaug, qa, vt, middle_s, ffn_in, act, rate,
            back_s, low_grad, low, dmix, dpl, whole, into, into2, arrived,
            kta, qm, doa, dom, delta, dk, dv, dqt, *own,
        ) = refs[17:]
        if begun:
            u_all, grad_s, branch_s, act_grad = [ref.get() for ref in begun_refs]
        else:
            u_all, grad_s, branch_s = own
        s = idx_ref[0]
        mine = idx_ref[1]
        dpre, dqkv = rate, qkv
        loads = []
        for k in range(len(given)):
            place = u_all.at[rows_at((s ^ k) * third, third), :]
            loads.append(pltpu.make_async_copy(given_refs[k], place, arrived.at[k]))
            loads[-1].start()
        for k in range(n):
            pooled_s[rows_at((s ^ k) * third, third), :] = pool_refs[k][0:third, :].astype(F32)
            carry[s ^ k] = pool_refs[k][third:, :].astype(F32)
        for j in range(1, n):
            pooled_s[j * third : j * third + 1, :] += carry[j - 1, 0:1, :]
        norm_into(Rows(length, lambda tile: pooled_s[tile, :]), ln_ref[2:3, :], ln_ref[6:7, :], attn)
        wq = wq.get()
        for c in range(0, 3 * d, 256):
            qkv[:, c : c + 256] = mm(attn[...], wq[:, c : c + 256]).astype(BF)

        def again(t):
            lane = pl.multiple_of(t * width, 128)
            own = t if kept_pairs > 1 else 0
            place_positions(kaug.at[own], width)
            prepare(
                qkv[:, pl.ds(lane, width)],
                qkv[:, pl.ds(d + lane, width)],
                [slope_ref[1, 2 * t + h] for h in range(2)],
                kaug.at[own],
                qa.at[own],
            )
            return kaug.at[own], qa.at[own]

        def forward(t, _):
            lane = pl.multiple_of(t * width, 128)
            own_kaug, own_qa = again(t)
            vt[...] = flip(qkv[:, pl.ds(2 * d + lane, width)]).astype(BF)
            attend(own_kaug, own_qa, vt, mixt.at[t], lse.at[t], 2)
            mixed[:, pl.ds(lane, width)] = flip(mixt[t].astype(BF))
            return 0

        lax.fori_loop(0, pairs, forward, 0)
        wo = wo.get()
        middle_s[...] = pooled_s[...] + mm(mixed[...], wo[...])
        norm_into(Rows(length, lambda tile: middle_s[tile, :]), ln_ref[3:4, :], ln_ref[7:8, :], ffn_in)
        wi, wb = wi.get(), wb.get()
        ffn_forward(ffn_in, wi, bi, act, rate, length, ff)
        low[...] = (middle_s[...] + bb[0:1, :] + mm(act[...], wb[...])).astype(BF)
        mine_rows = rows_at(s * third, third)
        own = low[mine_rows, :]
        wu, full = wu.get(), fg.get()
        for c in range(3):
            part = slice(c * d, (c + 1) * d)
            up = mm(own, wu[:, part]) + bu[0:1, part]
            spread(whole, c, full[:, part] + up)
        for l in range(d // 128):
            block_out.ref[:, l * 128 : (l + 1) * 128] = whole[l].astype(BF)
        block_out.send()

        small = small.ref
        small[...] = jnp.zeros_like(small)
        for load in loads:
            load.wait()
        u = u_all[...]
        if not begun:
            grad_s[...] = nt(u, wu[...])
            branch_s[...] = grad_s[...].astype(BF)
        small[1:2, 0 : 3 * d] = jnp.sum(u.astype(F32), axis=0, keepdims=True)
        small[3:4, 0:d] = jnp.sum(branch_s[...].astype(F32), axis=0, keepdims=True)
        if begun:
            for lanes in tiles(ff, 512):
                value = (act_grad[:, lanes].astype(F32) * rate[:, lanes].astype(F32)).astype(BF)
                dpre[:, lanes] = value
                small[0:1, lanes] = jnp.sum(value.astype(F32), axis=0, keepdims=True)
        else:
            ffn_backward(branch_s, wb, rate, dpre, small.at[0:1, :], length, ff)
        back_s[...] = nt(dpre[...], wi[...])

        def put_middle(tile, value):
            value = grad_s[tile, :] + value
            grad_s[tile, :] = value
            low_grad[tile, :] = value.astype(BF)

        gain_late, bias_late = norm_back(
            lambda tile: middle_s[tile, :], ln_ref[3:4, :], lambda tile: back_s[tile, :], put_middle, length
        )
        dmix[...] = nt(low_grad[...], wo[...]).astype(BF)

        def backward(t, slope_row):
            lane = pl.multiple_of(t * width, 128)
            prepare_back(
                qkv[:, pl.ds(lane, width)],
                qkv[:, pl.ds(d + lane, width)],
                dmix[:, pl.ds(lane, width)],
                mixt.at[t],
                kta,
                qm,
                doa,
                dom,
                delta,
                2,
            )
            own_kaug, own_qa = (kaug.at[t], qa.at[t]) if kept_pairs > 1 else again(t)
            vt2 = qkv.at[:, pl.ds(2 * d + lane, width)]
            sums = attend_back(
                own_kaug, own_qa, vt2, kta, qm, doa, dom, delta, lse.at[t], dk, dv, dqt, 2
            )
            dqkv[:, pl.ds(lane, width)] = flip(dqt[...].astype(BF))
            dqkv[:, pl.ds(d + lane, width)] = dk[...].astype(BF)
            dqkv[:, pl.ds(2 * d + lane, width)] = dv[...].astype(BF)
            for h in range(2):
                slope_row = slope_row + lone(jnp.sum(sums[h], axis=1, keepdims=True), 2 * t + h)
            return slope_row

        slope_row = lax.fori_loop(0, pairs, backward, jnp.zeros((1, 128), F32))
        small[3:4, d : d + 128] = slope_row
        back_s[...] = nt(dqkv[...], wq[...])

        def put_pooled(tile, value):
            dpl[0, tile, :] = (grad_s[tile, :] + value).astype(BF)

        gain_early, bias_early = norm_back(
            lambda tile: pooled_s[tile, :], ln_ref[2:3, :], lambda tile: back_s[tile, :], put_pooled, length
        )
        wide = dpl[0].astype(F32)
        small[2:3, 0:d] = gain_early
        small[2:3, d : 2 * d] = gain_late
        small[2:3, 2 * d : 3 * d] = bias_early
        small[2:3, 3 * d : 4 * d] = bias_late
        small[1:2, 3 * d : 4 * d] = jnp.sum(wide, axis=0, keepdims=True)
        later = pltpu.roll(wide, length - 1, 0)
        dpl[1] = jnp.where(iota((length, d), 0) == length - 1, 0.0, later).astype(BF)
        here, after = dpl[0, mine_rows, :], dpl[1, mine_rows, :]
        pair.ref[...] = dpl[...]
        wp = wp.get()
        given_own = u_all[mine_rows, :].astype(F32)
        spread(whole, 0, given_own[:, 0:d] + nt(here, wp[2 * d :, :]))
        spread(whole, 1, given_own[:, d : 2 * d] + nt(after, wp[0:d, :]))
        spread(whole, 2, given_own[:, 2 * d :] + nt(after, wp[d : 2 * d, :]))
        for l in range(d // 128):
            full_grad.ref[:, l * 128 : (l + 1) * 128] = whole[l]
        full_grad.send()

        def put(name, block, value):
            at, count, _ = spans[name]
            at += block * count
            into[...] = flip(value.astype(BF))
            for far in range(m // 2):
                for bit, target in ((0, keep), (1, give)):
                    start = (mine ^ (2 * far + bit)) * count
                    target[far, at : at + count, :] = into[rows_at(start, count), :]

        def put_tall(name, value):
            at, count, _ = spans[name]
            into2[...] = flip(value.astype(BF))
            for far in range(m // 2):
                for bit, target in ((0, keep), (1, give)):
                    start = (mine ^ (2 * far + bit)) * count
                    target[far, at : at + count, :] = into2[rows_at(start, count), :]

        put_tall("qkv", tn(lanes_at(attn, s * kw, kw), dqkv[...]))
        put("out", 0, tn(lanes_at(mixed, s * kw, kw), low_grad[...]))
        at, count, blocks = spans["in"]
        grad_in = tn(lanes_at(ffn_in, s * kw, kw), dpre[...]).astype(BF)
        for b in range(m):
            for i in range(blocks):
                first = (b * blocks + i) * kw
                here = slice(at + i * count, at + (i + 1) * count)
                piece = grad_in[:, first : first + kw]

                def store(target, far=(mine ^ b) >> 1, here=here, piece=piece):
                    target[far, here, :] = piece

                pl.when(((mine ^ b) & 1) == 0)(lambda: store(keep))
                pl.when(((mine ^ b) & 1) == 1)(lambda: store(give))
        blocks = spans["back"][2]
        for i in range(blocks):
            put("back", i, tn(lanes_at(act, (s * blocks + i) * kw, kw), branch_s[...]))
        put_tall("up", tn(lanes_at(low, s * kw, kw), u))

    outs = [
        ((rows, d), BF, FAR),
        ((rows, d), F32, hold(n)),
        ((2, length, d), BF, hold(n)),
        ((m // 2, packed_rows, kw), BF),
        ((m // 2, packed_rows, kw), BF),
        ((8, ff), F32, hold(n)),
    ]
    scratch = [
        pltpu.VMEM((length, d), F32),
        pltpu.VMEM((n, CARRY, d), F32),
        pltpu.VMEM((length, d), BF),
        pltpu.VMEM((length, 3 * d), BF),
        pltpu.VMEM((length, d), BF),
        pltpu.VMEM((pairs, width, length), F32),
        pltpu.VMEM((pairs, 8, length), F32),
        *attend_scratch(length, width, 2, (kept_pairs,)),
        pltpu.VMEM((width, length), BF),
        pltpu.VMEM((length, d), F32),
        pltpu.VMEM((length, d), BF),
        pltpu.VMEM((length, ff), BF),
        pltpu.VMEM((length, ff), BF),
        pltpu.VMEM((length, d), F32),
        pltpu.VMEM((length, d), BF),
        pltpu.VMEM((length, d), BF),
        pltpu.VMEM((length, d), BF),
        pltpu.VMEM((2, length, d), BF),
        pltpu.VMEM((d // 128, rows, 128), F32),
        pltpu.VMEM((d, kw), BF),
        pltpu.VMEM((3 * d, kw), BF),
        pltpu.SemaphoreType.DMA((n,)),
        *back_scratch(length, width, 2),
    ]
    if not begun:
        scratch += [
            pltpu.VMEM((length, 3 * d), BF),
            pltpu.VMEM((length, d), F32),
            pltpu.VMEM((length, d), BF),
        ]
    return call(
        body,
        "short_layer",
        [idx, slopes, *pooled, *given, *begun, full_g, lnp, w_qkv, w_out, w_in, b_in, w_back, b_back, w_pool, w_up, b_up],
        [smem(), smem()]
        + [NEAR] * n
        + [anywhere()] * len(given)
        + [HELD] * len(begun)
        + [held(n), NEAR, *[HELD if begun else 1] * 3, NEAR, HELD if begun else 1, NEAR]
        + [HELD if begun else ALL] * 2
        + [NEAR],
        outs,
        scratch,
        after=after,
        spare=4 if keeps(n) else 20,
    )


def core_columns(ref, width, core):
    total = ref.shape[1]
    if width % 128 == 0:
        starts = [pl.multiple_of((2 * z + core) * width, 128) for z in range(total // width // 2)]
        return jnp.concatenate([ref[:, pl.ds(start, width)] for start in starts], axis=1)
    shape = (total, total // 2)
    row, column = iota(shape, 0), iota(shape, 1)
    block = lax.div(column, width)
    pick = row == (2 * block + core) * width + (column - block * width)
    return mm(ref[...], pick.astype(F32).astype(BF)).astype(BF)


def first_ffn_back(idx, full_grad, mid, rate, forward, lnp, w_out, w_in, w_back, fetch, n, m):
    rows, d = mid.shape
    ff = rate.shape[1]
    dh = d // n

    def body(*refs):
        idx_ref, grad_ref, mid_ref, rate_ref, forward_ref, ln_ref, wo, wi, wb = refs[:9]
        sources, refs = refs[9 : 9 + len(fetch)], refs[9 + len(fetch) :]
        sends, refs = refs[:n], refs[n:]
        middle_grad, own, give, small = refs[:4]
        targets, refs = refs[4 : 4 + len(fetch)], refs[4 + len(fetch) :]
        dpre, low_ref, branch_ref, back_s, fetched = refs
        loads = [
            pltpu.make_async_copy(source, target.ref, fetched.at[i])
            for i, (source, target) in enumerate(zip(sources, targets))
        ]
        for load in loads:
            load.start()
        s, core = idx_ref[0], idx_ref[1] & 1
        grad = grad_ref.get()[...]
        branch = grad.astype(BF)
        branch_ref[...] = branch
        sums = small.ref
        sums[...] = jnp.zeros_like(sums)
        sums[5:6, 2 * d : 3 * d] = jnp.sum(branch.astype(F32), axis=0, keepdims=True)
        wb, wi, rates = wb.get(), wi.get(), rate_ref.get()
        ffn_backward(branch_ref, wb, rates, dpre, sums.at[4:5, :], rows, ff)
        back_s[...] = nt(dpre[...], wi[...])
        middles, grads = mid_ref.get(), grad_ref.get()

        def put(tile, value):
            value = grads[tile, :] + value
            middle_grad.ref[tile, :] = value
            low_ref[tile, :] = value.astype(BF)

        gain, bias = norm_back(
            lambda tile: middles[tile, :], ln_ref[1:2, :], lambda tile: back_s[tile, :], put, rows
        )
        sums[5:6, 0:d] = gain
        sums[5:6, d : 2 * d] = bias
        small.send()
        middle_grad.send()
        wo = wo.get()
        for k in range(n):
            sends[k][0:rows, :] = nt(low_ref[...], wo[rows_at((s ^ k) * dh, dh), :]).astype(BF)
        groups = forward_ref.get().at[rows:, 0 : 3 * d]
        third = rows // 3
        for k in range(n):
            for i in range(3):
                _, start = pool_unit(3 * (s ^ k) + i, n, d)
                sends[k][rows + i * third : rows + (i + 1) * third, :] = lanes_at(groups, start, dh)
        for target, bit in ((own, 0), (give, 1)):
            target.ref[0:rows, 0 : ff // 2] = core_columns(dpre, ff // m, core ^ bit)
            target.ref[0:rows, ff // 2 : (ff + d) // 2] = core_columns(branch_ref, d // m, core ^ bit)
            target.ref[0:rows, (ff + d) // 2 :] = core_columns(low_ref, d // m, core ^ bit)
        for load in loads:
            load.wait()

    pack = (rows, ff // 2 + d)
    outs = [((2 * rows, dh), BF)] * n + [
        ((rows, d), F32, hold(n)),
        (pack, BF, hold(n)),
        (pack, BF, hold(n)),
        ((8, ff), F32, hold(n)),
        *[(array.shape, array.dtype, HOLD) for array in fetch],
    ]
    weight = HELD if keeps(n) else 0
    result = call(
        body,
        "first_ffn_back",
        [idx, full_grad, mid, rate, forward, lnp, w_out, w_in, w_back, *fetch],
        [smem()] + [held(n)] * 4 + [NEAR, weight, weight, weight] + [anywhere()] * len(fetch),
        outs,
        [pltpu.VMEM((rows, ff), BF), pltpu.VMEM((rows, d), BF), pltpu.VMEM((rows, d), BF)]
        + [pltpu.VMEM((rows, d), F32), pltpu.SemaphoreType.DMA((max(len(fetch), 1),))],
    )
    return result[:n], result[n:]


def halves(n, count):
    bits = [1 << t for t in range(n.bit_length() - 1)]
    return ((bits, range(0, count // 2)), (bits[::-1], range(count // 2, count)))


def kept_orders(n, bits):
    orders = [list(range(n))]
    for bit in bits:
        orders.append([r for r in orders[-1] if not r & bit])
    return orders


def first_ffn_weights(idx, forward, forward_other, back, back_other, n, m, d, ff, after):
    rows = forward.shape[0] // 4 * 3
    kw = d // n
    far = m // 2
    spans, packed_rows = ffn_layout(n, m, d, ff)
    plan = halves(n, far)

    def body(*refs):
        idx_ref, own_f, other_f, own_b, other_b = refs[:5]
        targets = refs[5:9]
        wide_in, wide_back, wide_out = refs[9:]
        s, mine = idx_ref[0], idx_ref[1]
        per, share, count_out = ff // m, ff // n, d // m
        f, g, b, h = own_f.get(), other_f.get(), own_b.get(), other_b.get()
        cut_in, cut_back = ff // 2, (ff + d) // 2
        turned = [flip(x[0:rows, ff : ff + d]).astype(BF) for x in (f, g)]
        for z in range(far):
            part = slice(z * per, (z + 1) * per)
            wide_in[z] = (mm(turned[0], b[0:rows, part]) + mm(turned[1], h[0:rows, part])).astype(BF)
        turned = [flip(x[0:rows, cut_in:cut_back]).astype(BF) for x in (b, h)]
        for j in range(n):
            part = slice(j * share, (j + 1) * share)
            wide_back[j] = (mm(turned[0], f[0:rows, part]) + mm(turned[1], g[0:rows, part])).astype(BF)
        turned = [flip(x[0:rows, cut_back:]).astype(BF) for x in (b, h)]
        for j in range(n):
            part = slice(ff + d + j * kw, ff + d + (j + 1) * kw)
            wide_out[j] = (mm(turned[0], f[0:rows, part]) + mm(turned[1], g[0:rows, part])).astype(BF)
        for half, (bits, places) in enumerate(plan):
            order = kept_orders(n, bits)[0]
            keeps_, gives = [r for r in order if not r & bits[0]], [r for r in order if r & bits[0]]
            for target, chosen in ((targets[2 * half], keeps_), (targets[2 * half + 1], gives)):
                first = 0
                for r in chosen:
                    j = s ^ r
                    for zr in places:
                        z = (mine >> 1) ^ zr
                        at, count, _ = spans["out"]
                        target[first + at : first + at + count, :] = wide_out[j, rows_at(z * count, count), :]
                        at, count, blocks = spans["in"]
                        for i in range(blocks):
                            target[first + at + i * count : first + at + (i + 1) * count, :] = wide_in[
                                z, rows_at(j * kw, kw), i * kw : (i + 1) * kw
                            ]
                        at, count, blocks = spans["back"]
                        for i in range(blocks):
                            target[first + at + i * count : first + at + (i + 1) * count, :] = wide_back[
                                j, rows_at(z * count, count), i * kw : (i + 1) * kw
                            ]
                        first += packed_rows

    outs = [((n // 2 * (far // 2) * packed_rows, kw), BF)] * 4
    scratch = [
        pltpu.VMEM((far, d, ff // m), BF),
        pltpu.VMEM((n, d // 2, ff // n), BF),
        pltpu.VMEM((n, d // 2, kw), BF),
    ]
    return call(
        body,
        "first_ffn_weights",
        [idx, forward, forward_other, back, back_other],
        [smem(), held(n), HELD if keeps(n) else LOAD, held(n), HELD if keeps(n) else LOAD],
        outs,
        scratch,
        after=after,
    )


SMALL = 16


def small_layout(m, kw, d, ff):
    places, row = {}, 0
    for name, size in (("in0", ff // m), ("in1", ff // m), ("up", 3 * d // m)):
        places[name] = (row, 0, size)
        row += -(-size // kw)
    for one, two in (
        ("gain00", "gain01"),
        ("gain10", "gain11"),
        ("bias00", "bias01"),
        ("bias10", "bias11"),
        ("back0", "back1"),
        ("pool", None),
    ):
        places[one] = (row, 0, d // m)
        if two:
            places[two] = (row, kw // 2, d // m)
        row += 1
    places["slopes"] = (row, 0, 0)
    return places


def first_attention_back(
    idx, slopes, qkv, attn, mixt, lse, grads, wq, lnp, small_short, small_ffn, pooled_grad, head_count, dh, m, after
):
    n = len(grads)
    length, d = attn.shape
    rows = length // n
    third = rows // 3
    width = wq.shape[1] // 3
    kw = d // n
    ff = small_ffn.shape[1]
    heads = slopes.shape[1]

    def body(*refs):
        idx_ref, slope_ref, qkv_ref, attn_ref, mixt_ref, lse_ref = refs[:6]
        grad_refs = refs[6 : 6 + n]
        w_ref, ln_ref, short_ref, ffn_ref, pooled_ref = refs[6 + n : 11 + n]
        refs = refs[11 + n :]
        shares, sends, pool = refs[:n], refs[n : 2 * n], refs[2 * n]
        kaug, qa, do, turned, owners, table, groups, kta, qm, doa, dom, delta, dk, dv, dqt = refs[2 * n + 1 :]
        s = idx_ref[0]
        if dh < width:
            do[...] = jnp.zeros_like(do)
            dqt[...] = jnp.zeros_like(dqt)
        for k in range(n):
            do[rows_at((s ^ k) * rows, rows), 0:dh] = grad_refs[k][0:rows, :]
            for i in range(3):
                here = slice(rows + i * third, rows + (i + 1) * third)
                groups[i, rows_at((s ^ k) * third, third), :] = grad_refs[k][here, :]
        place_positions(kaug, width)
        qkv_ref = qkv_ref.get()
        q, k_ = qkv_ref[:, 0:width], qkv_ref[:, width : 2 * width]
        prepare(q, k_, [slope_ref[0, s * head_count + h] for h in range(head_count)], kaug, qa)
        prepare_back(q, k_, do[...], mixt_ref.get(), kta, qm, doa, dom, delta, head_count)
        sums = attend_back(
            kaug, qa, qkv_ref.at[:, 2 * width :], kta, qm, doa, dom, delta, lse_ref.get(), dk, dv, dqt, head_count
        )
        turned[0:width, :] = dqt[...].astype(BF)
        turned[width : 2 * width, :] = flip(dk[...].astype(BF))
        turned[2 * width :, :] = flip(dv[...].astype(BF))
        do[...] = flip(dqt[...].astype(BF))
        for k in range(n):
            here = rows_at((s ^ k) * rows, rows)
            sends[k][0:rows, :] = do[here, 0:dh]
            sends[k][rows : 2 * rows, :] = dk[here, 0:dh].astype(BF)
            sends[k][2 * rows : 3 * rows, :] = dv[here, 0:dh].astype(BF)
        grad_w = mm(turned[...], attn_ref.get()[...])
        for j in range(n):
            for g in range(3):
                owners[j, g * dh : (g + 1) * dh, :] = grad_w[
                    g * width : g * width + dh, j * kw : (j + 1) * kw
                ].astype(BF)
        w_turned = flip(w_ref.get()[...]).astype(F32)
        gain, bias = ln_ref[0:1, :], ln_ref[4:5, :]
        column = jnp.sum(turned[...].astype(F32), axis=1, keepdims=True)
        bias_grad = jnp.sum(w_turned * column, axis=0, keepdims=True)
        gain_grad = (jnp.sum(w_turned * grad_w, axis=0, keepdims=True) - bias * bias_grad) / gain
        once = jnp.where(s == 0, 1.0, 0.0)
        both = ffn_ref.get()[...] + once * short_ref.get()[...]
        slope_row = jnp.zeros((1, 128), F32)
        for h in range(head_count):
            slope_row = slope_row + lone(jnp.sum(sums[h], axis=1, keepdims=True), s * head_count + h)
        table[...] = jnp.zeros_like(table)
        vectors = {
            "in0": both[4:5, :],
            "in1": both[0:1, :],
            "up": both[1:2, 0 : 3 * d],
            "gain00": gain_grad,
            "gain01": both[5:6, 0:d],
            "gain10": both[2:3, 0:d],
            "gain11": both[2:3, d : 2 * d],
            "bias00": bias_grad,
            "bias01": both[5:6, d : 2 * d],
            "bias10": both[2:3, 2 * d : 3 * d],
            "bias11": both[2:3, 3 * d : 4 * d],
            "back0": both[5:6, 2 * d : 3 * d],
            "back1": both[3:4, 0:d],
            "pool": both[1:2, 3 * d : 4 * d],
        }
        for name, (row, lane, size) in small_layout(m, kw, d, ff).items():
            for b in range(m):
                if name == "slopes":
                    table[b * SMALL + row : b * SMALL + row + 1, 0:heads] = slope_row[:, 0:heads]
                    table[b * SMALL + row : b * SMALL + row + 1, heads : 2 * heads] = both[3:4, d : d + heads]
                    continue
                for at in range(0, size, kw):
                    span = min(kw, size - at)
                    spot = b * SMALL + row + at // kw
                    first = b * size + at
                    table[spot : spot + 1, lane : lane + span] = vectors[name][:, first : first + span]
        pooled_ref = pooled_ref.get()
        for i in range(3):
            early, _ = pool_unit(3 * s + i, n, d)
            pool[i * d : (i + 1) * d, :] = flip(tn(groups[i], pooled_ref[early.astype(jnp.int32)]).astype(BF))
        for k in range(n):
            shares[k][0 : 3 * dh, :] = owners[s ^ k]
            shares[k][3 * dh :, :] = table[...].astype(BF)

    outs = [((3 * dh + m * SMALL, kw), BF)] * n + [((3 * rows, dh), BF)] * n + [((3 * d, kw), BF)]
    scratch = (
        attend_scratch(length, width, head_count)
        + [
            pltpu.VMEM((length, width), BF),
            pltpu.VMEM((3 * width, length), BF),
            pltpu.VMEM((n, 3 * dh, kw), BF),
            pltpu.VMEM((m * SMALL, kw), F32),
            pltpu.VMEM((3, n * third, kw), BF),
        ]
        + back_scratch(length, width, head_count)
    )
    result = call(
        body,
        "first_attention_back",
        [idx, slopes, qkv, attn, mixt, lse, *grads, wq, lnp, small_short, small_ffn, pooled_grad],
        [smem(), smem()] + [held(n)] * 4 + [NEAR] * n + [ALL, NEAR, held(n), held(n), held(n)],
        outs,
        scratch,
        after=after,
    )
    return result[:n], result[n : 2 * n], result[2 * n]


def input_gradient(idx, pieces, w_qkv, hid, middle_grad, lnp, after):
    n = len(pieces)
    dh = pieces[0].shape[1]
    rows, d = hid.shape

    def body(*refs):
        idx_ref = refs[0]
        piece_refs = refs[1 : 1 + n]
        w_ref, hid_ref, mid_ref, ln_ref, out, owners, whole, back = refs[1 + n :]
        s = idx_ref[0]
        for k in range(n):
            owners[s ^ k] = piece_refs[k][0 : 3 * rows, :]
        for j in range(n):
            for g in range(3):
                whole[:, g * d + j * dh : g * d + (j + 1) * dh] = owners[j, g * rows : (g + 1) * rows, :]
        back[...] = nt(whole[...], w_ref.get()[...])
        hid_ref, mid_ref = hid_ref.get(), mid_ref.get()

        def put(tile, value):
            out.ref[tile, :] = mid_ref[tile, :] + value

        norm_back(
            lambda tile: hid_ref[tile, :].astype(F32), ln_ref[0:1, :], lambda tile: back[tile, :], put, rows
        )

    scratch = [pltpu.VMEM((n, 3 * rows, dh), BF), pltpu.VMEM((rows, 3 * d), BF), pltpu.VMEM((rows, d), F32)]
    return call(
        body,
        "input_gradient",
        [idx, *pieces, w_qkv, hid, middle_grad, lnp],
        [smem()] + [NEAR] * n + [0, ALL, held(n), NEAR],
        [((rows, d), F32, FAR)],
        scratch,
        after=after,
        weight=0,
    )[0]


def order_shares(idx, pieces, pool, m, d, after):
    n = len(pieces)
    kw = pieces[0].shape[1]
    per, block, blocks = last_layout(n, m, d)
    every = per + block * blocks + SMALL
    dh = kw

    def body(*refs):
        idx_ref = refs[0]
        piece_refs = refs[1 : 1 + n]
        pool_ref, keep, give_near, give_far, natural, table = refs[1 + n :]
        s, mine = idx_ref[0], idx_ref[1]
        total = jnp.zeros((m * SMALL, kw), F32)
        for k in range(n):
            for g in range(3):
                at = g * dh
                natural[rows_at(g * d + (s ^ k) * dh, dh), :] = piece_refs[k][at : at + dh, :]
            total = total + piece_refs[k][3 * dh :, :].astype(F32)
        table[...] = total.astype(BF)
        for rel in range(m):
            target = (give_far if rel >= m // 2 else give_near) if rel & 1 else keep
            at = ((rel >> 1) % (m // 4) if rel & 1 else rel >> 1) * every
            b = mine ^ rel
            target[at : at + per, :] = natural[rows_at(b * per, per), :]
            for i in range(blocks):
                here = slice(at + per + i * block, at + per + (i + 1) * block)
                target[here, :] = pool_ref[rows_at(i * d + b * block, block), :]
            target[at + every - SMALL : at + every, :] = table[rows_at(b * SMALL, SMALL), :]

    return call(
        body,
        "order_shares",
        [idx, *pieces, pool],
        [smem()] + [NEAR] * (n + 1),
        [((m // 2 * every, kw), BF)] + [((m // 4 * every, kw), BF)] * 2,
        [pltpu.VMEM((3 * d, kw), BF), pltpu.VMEM((m * SMALL, kw), BF)],
        after=after,
    )


def unpack(held, spans, which, kw, n, qkv, out, inner, back):
    for j in range(n):
        lanes = slice(j * kw, (j + 1) * kw)
        for name, target in (("qkv", qkv), ("out", out)):
            at, count, _ = spans[name]
            target[:, lanes] = held[j, at : at + count, :].astype(F32)
        at, count, blocks = spans["in"]
        for i in range(blocks):
            inner[lanes, i * kw : (i + 1) * kw] = held[j, at + i * count : at + (i + 1) * count, :].astype(F32)
        at, count, blocks = spans["back"]
        for i in range(blocks):
            first = (j * blocks + i) * kw
            back[:, first : first + kw] = held[j, at + i * count : at + (i + 1) * count, :].astype(F32)


def both_layers(n, m, d, ff, which):
    shapes = ((2, 3 * d // m, d), (2, d // m, d), (2, d, ff // m), (2, d // m, ff))
    return [(shape, F32, PART, which) for shape in shapes]


def finish_short(idx, parts, skip, small, n, m, d, ff, heads, after):
    kw = d // n
    spans, _ = short_layout(n, m, d, ff)

    def body(*refs):
        idx_ref, part_refs, small = refs[0], refs[1 : 1 + n], refs[1 + n]
        qkv, out, inner, back, up = refs[2 + n : 7 + n]
        gains, biases, slopes, in_bias, back_bias, pool_bias, up_bias, held = refs[7 + n :]
        s = idx_ref[0]
        for k in range(n):
            held[s ^ k] = part_refs[k][skip if k else 0 :, :]
        unpack(held, spans, 1, kw, n, qkv.ref, out.ref, inner.ref, back.ref)
        for target in (qkv, out, inner, back):
            target.send()
        for j in range(n):
            at, count, _ = spans["up"]
            up.ref[:, j * kw : (j + 1) * kw] = held[j, at : at + count, :].astype(F32)
        up.send()
        places = small_layout(m, kw, d, ff)

        def pick(name, count):
            row, lane, _ = places[name]
            return small[row : row + 1, lane : lane + count]

        for which in range(2):
            for norm_at in range(2):
                name = str(which) + str(norm_at)
                gains[which, norm_at : norm_at + 1, :] = pick("gain" + name, d // m)
                biases[which, norm_at : norm_at + 1, :] = pick("bias" + name, d // m)
            back_bias[which : which + 1, :] = pick("back" + str(which), d // m)
            row = places["slopes"][0]
            slopes[which : which + 1, :] = small[row : row + 1, which * heads : (which + 1) * heads]
        pool_bias[...] = pick("pool", d // m)
        for at in range(0, ff // m, kw):
            for which in range(2):
                row = places["in" + str(which)][0] + at // kw
                in_bias[which : which + 1, at : at + kw] = small[row : row + 1, :]
        for at in range(0, 3 * d // m, kw):
            span = min(kw, 3 * d // m - at)
            row = places["up"][0] + at // kw
            up_bias[:, at : at + span] = small[row : row + 1, 0:span]

    outs = both_layers(n, m, d, ff, 1) + [
        ((3 * d // m, d), F32, FAR),
        ((2, 2, d // m), F32),
        ((2, 2, d // m), F32),
        ((2, heads), F32),
        ((2, ff // m), F32),
        ((2, d // m), F32),
        ((1, d // m), F32),
        ((1, 3 * d // m), F32),
    ]
    return call(
        body,
        "finish_short",
        [idx, *parts, small],
        [smem()] + [NEAR] * (n + 1),
        outs,
        [pltpu.VMEM((n,) + parts[0].shape, BF)],
        after=after,
        weight=0,
    )


def finish_first(idx, parts, begun, n, m, d, ff):
    kw = d // n
    spans, rows = ffn_layout(n, m, d, ff)
    per, block, blocks = last_layout(n, m, d)
    spans = dict(spans, qkv=(rows, per, 1), pool=(rows + per, block, blocks))

    def body(*refs):
        idx_ref, part_refs = refs[0], refs[1 : 1 + n]
        qkv, out, inner, back, pool, held = refs[5 + n :]
        s = idx_ref[0]
        for k in range(n):
            held[s ^ k] = part_refs[k][...]
        unpack(held, spans, 0, kw, n, qkv.ref, out.ref, inner.ref, back.ref)
        for target in (qkv, out, inner, back):
            target.send()
        for j in range(n):
            at, count, blocks = spans["pool"]
            for i in range(blocks):
                first = (j * blocks + i) * kw
                pool.ref[:, first : first + kw] = held[j, at + i * count : at + (i + 1) * count, :].astype(F32)
        pool.send()

    outs = both_layers(n, m, d, ff, 0) + [((d // m, 3 * d), F32, FAR)]
    return call(
        body,
        "finish_first",
        [idx, *parts, *begun],
        [smem()] + [NEAR] * n + [RAW] * 4,
        outs,
        [pltpu.VMEM((n,) + parts[0].shape, BF)],
        aliases={n + 1 + i: i for i in range(4)},
    )


def swap(array, axis, by):
    count = lax.axis_size(axis)
    return lax.ppermute(array, axis, [(i, i ^ by) for i in range(count)])


def gather(array, axis):
    return [array] + [swap(array, axis, k) for k in range(1, lax.axis_size(axis))]


def exchange(arrays, axis):
    return [arrays[0]] + [swap(arrays[k], axis, k) for k in range(1, len(arrays))]


def local(
    hidden_in, out_grad, start_flags, ln_gain, ln_bias, w_qkv, w_out, slopes, w_in, b_in, w_back, b_back,
    w_pool, b_pool, w_up, b_up,
):
    n, m = lax.axis_size("seq"), lax.axis_size("batch")
    s, mine = lax.axis_index("seq"), lax.axis_index("batch")
    idx = jnp.stack([s, mine]).astype(jnp.int32)
    hid = hidden_in[0]
    rows, d = hid.shape
    ff = w_in.shape[2]
    heads = slopes.shape[1]
    head_count = heads // n
    dh = head_count * HEAD
    width = max(dh, 128)
    far = m // 2
    row = lambda v: v.astype(F32).reshape(1, -1)

    hidden_parts = gather(hid, "seq")
    lnp = jnp.concatenate([ln_gain.reshape(4, d), ln_bias.reshape(4, d)], axis=0).astype(F32)
    columns = [lax.dynamic_slice(w_qkv, (0, 0, g * d + s * dh), (1, d, dh))[0] for g in range(3)]
    wq = jnp.concatenate([jnp.pad(c, ((0, 0), (0, width - dh))) for c in columns], axis=1)
    early = first_rows([hid, hidden_parts[n - 1]], wq, lnp)
    given = mask_rows(out_grad[0], start_flags[0][:, None], [*hidden_parts[1:], early[1]])
    given_parts = [swap(given, "seq", k) for k in range(1, n - 1)]

    loaded = [(w_out, 0), (w_in, 0), (w_back, 0), (w_up, None), (w_back, 1)] if keeps(n) else []
    sends, (attn, qkv, mixt, lse), loaded = first_attention(
        idx, slopes, [None, *hidden_parts[1 : n - 1], None], early, wq, lnp, loaded, head_count, dh, [given]
    )
    fetched = loaded[3:]
    loaded = loaded[:3] or [w_out, w_in, w_back]
    mixes = exchange(sends, "seq")
    given = pass_on(given, [*mixes[1:], *given_parts])
    last_given = swap(given, "seq", n - 1)
    full_g, pooled, mid, forward, rate = first_ffn(
        idx, hid, mixes, lnp, loaded[0], loaded[1], row(b_in[0]), loaded[2], row(b_back[0]), w_pool, row(b_pool),
        [given],
    )
    pooled_parts = gather(pooled, "seq")
    forward_other = swap(forward, "batch", 1)
    given_parts = [given] + given_parts + [last_given]
    begun, up_held, back_held, short_weights = [], w_up, w_back, [w_qkv, w_out, w_in, w_pool]
    if keeps(n):
        up_held, back_held = fetched
        result = short_start(idx, given_parts, up_held, back_held, short_weights[:3], w_pool, [mid])
        begun, short_weights = result[:4], result[4:]
    block_out, full_grad, pair, keep, give, small_short = short_layer(
        idx, slopes, pooled_parts, given_parts, begun, full_g, lnp, *short_weights[:3], row(b_in[1]), back_held,
        row(b_back[1]), short_weights[3], up_held, row(b_up), m, [],
    )

    short_rows = keep.shape[1]
    keep, give = keep.reshape(-1, keep.shape[2]), give.reshape(-1, keep.shape[2])
    other = swap(give, "batch", 1)
    sends, (middle_grad, back, give, small_ffn, *fetched) = first_ffn_back(
        idx, full_grad, mid, rate, forward, lnp, *loaded, [forward_other] if keeps(n) else [], n, m
    )
    forward_other = fetched[0] if fetched else forward_other
    back_other = swap(give, "batch", 1)
    grads = exchange(sends, "seq")

    def split(parts, count, size, places):
        return [
            (BF, [[(part, i * size, size) for part in parts] for i in range(count) if places(i)]),
            (BF, [[(part, i * size, size) for part in parts] for i in range(count) if not places(i)]),
        ]

    even = lambda i: i % 2 == 0
    packs = first_ffn_weights(idx, forward, forward_other, back, back_other, n, m, d, ff, [])
    short_keep, short_give = fold("short_chip", split([keep, other], far, short_rows, even), [packs[0]])
    short_other = swap(short_give, "batch", 2)
    plan = halves(n, far)
    others = [swap(packs[2 * half + 1], "seq", bits[0]) for half, (bits, _) in enumerate(plan)]
    packs = [packs[0], packs[2]]
    shares, sends, pool = first_attention_back(
        idx, slopes, qkv, attn, mixt, lse, grads, wq, lnp, small_short, small_ffn, pair, head_count, dh, m, [short_keep]
    )
    shares = exchange(shares, "seq")

    size = ffn_layout(n, m, d, ff)[1]
    steps = n.bit_length() - 1
    short_count, after = far // 2, [shares[0]]
    for step in range(1, steps):
        targets, rest = [], []
        for (bits, places), pack, other in zip(plan, packs, others):
            orders = kept_orders(n, bits)[step]
            per = len(places) * size
            keeping = [i for i, r in enumerate(orders) if not r & bits[step]]
            targets += split([pack, other], len(orders), per, lambda i: i in keeping)
        if short_count > 1:
            targets += split([short_keep, short_other], short_count, short_rows, even)
        result = fold("first_plane", targets, after)
        packs, others = [result[0], result[2]], [result[1], result[3]]
        others = [swap(other, "seq", bits[step]) for (bits, _), other in zip(plan, others)]
        if short_count > 1:
            short_keep, short_other = result[4], swap(result[5], "batch", 2 * far // short_count)
            short_count //= 2
        after = [result[0]]
    while short_count > 1:
        short_keep, short_give = fold("short_plane", split([short_keep, short_other], short_count, short_rows, even))
        short_other = swap(short_give, "batch", 2 * far // short_count)
        short_count //= 2

    keep, *gives = order_shares(idx, shares, pool, m, d, after)
    last_rows = keep.shape[0] // far
    last_other = [swap(give, "batch", 1) for give in gives]
    short_sum = [(short_keep, 0, short_rows), (short_other, 0, short_rows)]

    def plane(z):
        half = z // (far // 2)
        at = (z - half * (far // 2)) * size
        return [(packs[half], at, size), (others[half], at, size)]

    def pieces(z):
        return [plane(z), [(keep, z * last_rows, last_rows), (last_other[2 * z // far], z % (far // 2) * last_rows, last_rows)]]

    short_total, result_keep, result_give, *messages = fold(
        "short_total",
        [(BF, [short_sum])]
        + [(BF, [block for z in range(far) if z % 2 == odd for block in pieces(z)]) for odd in range(2)]
        + [(BF, [[(sends[k], 0, sends[k].shape[0])], short_sum]) for k in range(1, n)],
        [keep],
    )
    both, count = size + last_rows, far // 2
    other = swap(result_give, "batch", 2)
    messages = [swap(message, "seq", k + 1) for k, message in enumerate(messages)]
    while count > 1:
        blocks = [[(part, i * both, both) for part in (result_keep, other)] for i in range(count)]
        result_keep, result_give = fold(
            "last_plane",
            [(BF, [blocks[i] for i in range(count) if i % 2 == odd]) for odd in range(2)],
            weight=0,
        )
        other = swap(result_give, "batch", 2 * far // count)
        count //= 2
    count = both - SMALL
    parts = [result_keep, other]
    first_total, smalls = fold(
        "first_total",
        [(BF, [[(part, 0, count) for part in parts]]), (F32, [[(part, count, SMALL) for part in parts]])],
        weight=0,
    )
    first_parts = gather(first_total, "seq")
    hidden_grad = input_gradient(idx, [sends[0], *messages], w_qkv, hid, middle_grad, lnp, [first_total])
    short_parts = [short_total, *messages]
    *begun, g_up, gains, biases, slope_grad, in_bias, back_bias, pool_bias, up_bias = finish_short(
        idx, short_parts, sends[0].shape[0], smalls, n, m, d, ff, heads, [in_hbm(hidden_grad)]
    )
    g_qkv, g_out, g_in, g_back, g_pool = finish_first(idx, first_parts, begun, n, m, d, ff)
    turn = lambda a: jnp.swapaxes(a, -1, -2)
    return (
        block_out[None],
        hidden_grad[None],
        gains,
        biases,
        turn(g_qkv),
        turn(g_out),
        slope_grad,
        g_in,
        in_bias,
        turn(g_back),
        back_bias,
        turn(g_pool),
        pool_bias[0],
        turn(g_up),
        up_bias[0],
    )


def solution(mesh):
    rows = P("batch", "seq", None)
    last = P(None, None, "batch")
    in_specs = (rows, rows, P("batch", "seq")) + (P(),) * 13
    out_specs = (
        rows,
        rows,
        last,
        last,
        last,
        last,
        P(),
        last,
        P(None, "batch"),
        last,
        P(None, "batch"),
        P(None, "batch"),
        P("batch"),
        P(None, "batch"),
        P("batch"),
    )
    return jax.shard_map(local, mesh=mesh, in_specs=in_specs, out_specs=out_specs, check_vma=False)
```

```python
import jax
import jax.numpy as jnp
from jax import lax
from jax.experimental import pallas as pl
from jax.experimental.pallas import tpu as pltpu
from jax.sharding import PartitionSpec as P

EPSILON = 1e-05
NEGATIVE = -1e30
HEAD = 64
SCALE = HEAD ** (-0.5)
POS = 128
BQ = 256
F32 = jnp.float32
BF = jnp.bfloat16
VMEM_LIMIT = 60 * 1024 * 1024
GELU_A = 0.7978845608028654
GELU_B = 0.044715


def dims(a, b, ca, cb):
    return lax.dot_general(a, b, (((ca,), (cb,)), ((), ())), preferred_element_type=F32)


def mm(a, b):
    return dims(a, b, 1, 0)


def nt(a, b):
    return dims(a, b, 1, 1)


def tn(a, b):
    return dims(a, b, 0, 0)


def flip(a):
    return jnp.transpose(a)


def iota(shape, axis):
    return lax.broadcasted_iota(jnp.int32, shape, axis)


def standard(x):
    centred = x - jnp.mean(x, axis=-1, keepdims=True)
    rstd = lax.rsqrt(jnp.mean(centred * centred, axis=-1, keepdims=True) + EPSILON)
    return centred * rstd, rstd


TILE = 64


def tiles(rows, size):
    return [slice(at, min(at + size, rows)) for at in range(0, rows, size)]


def norm_into(source, gain, bias, target, first=0):
    rows = source.rows
    for tile in tiles(rows, TILE):
        target[pl.ds(first + tile.start, tile.stop - tile.start), :] = (
            standard(source(tile))[0] * gain + bias
        ).astype(BF)


class Rows:
    def __init__(self, rows, read):
        self.rows, self.read = rows, read

    def __call__(self, tile):
        return self.read(tile)


def norm_back(x, gain, grad, put, rows):
    gain_sum = bias_sum = None
    for tile in tiles(rows, TILE):
        xhat, rstd = standard(x(tile))
        given = grad(tile)
        inner = given * gain
        put(
            tile,
            rstd
            * (
                inner
                - jnp.mean(inner, axis=-1, keepdims=True)
                - xhat * jnp.mean(inner * xhat, axis=-1, keepdims=True)
            ),
        )
        one = jnp.sum(given * xhat, axis=0, keepdims=True)
        two = jnp.sum(given, axis=0, keepdims=True)
        gain_sum = one if gain_sum is None else gain_sum + one
        bias_sum = two if bias_sum is None else bias_sum + two
    return gain_sum, bias_sum


def ffn_forward(normal, w_in, b_in, act, rate, rows, ff):
    for lanes in tiles(ff, 256):
        for tile in tiles(rows, 128):
            value, slope = gelu_both(mm(normal[tile, :], w_in[:, lanes]) + b_in[0:1, lanes])
            act[tile, lanes] = value.astype(BF)
            rate[tile, lanes] = slope.astype(BF)


def ffn_backward(branch, w_back, rate, dpre, sums, rows, ff):
    for lanes in tiles(ff, 512):
        value = (nt(branch[...], w_back[lanes, :]) * rate[:, lanes].astype(F32)).astype(BF)
        dpre[:, lanes] = value
        sums[:, lanes] = jnp.sum(value.astype(F32), axis=0, keepdims=True)


def gelu_both(x):
    square = x * x
    half = 0.5 * jnp.tanh(x * (GELU_A + GELU_A * GELU_B * square)) + 0.5
    value = x * half
    return value, half + (value - value * half) * (2.0 * GELU_A + 6.0 * GELU_A * GELU_B * square)


def rows_at(start, size):
    return pl.ds(pl.multiple_of(start, 16), size)


def lone(value, lane):
    return jnp.where(iota((1, 128), 1) == lane, value, 0.0)


def spread(target, first, value):
    for l in range(target.shape[0]):
        target[l, pl.ds(first, value.shape[0], stride=3), :] = value[:, l * 128 : (l + 1) * 128]


def lanes_at(ref, start, width):
    if width % 128 == 0:
        return ref[:, pl.ds(pl.multiple_of(start, 128), width)]
    total = ref.shape[1]
    pick = (iota((total, width), 0) == iota((total, width), 1) + start).astype(F32).astype(BF)
    return mm(ref[...], pick).astype(BF)


def place_positions(kaug, width):
    length = kaug.shape[0]
    row = iota((length, POS), 0)
    lane = iota((length, POS), 1)
    value = jnp.where(lane < 3, (row >> 7) << 7, jnp.where(lane < 6, row & 127, 0))
    kaug[:, width : width + POS] = value.astype(F32).astype(BF)


def slope_rows(slope, length):
    full = jnp.full((POS, length), slope, F32)
    first = full.astype(BF)
    rest = full - first.astype(F32)
    second = rest.astype(BF)
    third = (rest - second.astype(F32)).astype(BF)
    row = iota((POS, length), 0)
    part = jnp.where(
        (row == 0) | (row == 3),
        first.astype(F32),
        jnp.where(
            (row == 1) | (row == 4),
            second.astype(F32),
            jnp.where((row == 2) | (row == 5), third.astype(F32), 0.0),
        ),
    )
    return part.astype(BF)


def prepare(q, k, slopes, kaug, qa):
    length, width = q.shape
    kaug[:, 0:width] = k
    turned = flip(q) * SCALE
    row = iota((width, length), 0)
    for h, slope in enumerate(slopes):
        own = (row >= HEAD * h) & (row < HEAD * h + HEAD)
        qa[h, 0:width, :] = jnp.where(own, turned, 0.0).astype(BF)
        qa[h, width : width + POS, :] = slope_rows(slope, length)


def causal():
    return iota((BQ, BQ), 0) <= iota((BQ, BQ), 1)


def attend(kaug, qa, vt, mixt, lse, heads):
    length = kaug.shape[0]
    for i in range(length // BQ):
        here = slice(i * BQ, (i + 1) * BQ)
        spans = [slice(j * BQ, (j + 1) * BQ) for j in range(i + 1)]
        for h in range(heads):
            qh = qa[h, :, here]
            scores, top = [], None
            for span in spans:
                score = mm(kaug[span, :], qh)
                if span == here:
                    score = jnp.where(causal(), score, NEGATIVE)
                scores.append(score)
                one = jnp.max(score, axis=0, keepdims=True)
                top = one if top is None else jnp.maximum(top, one)
            own = slice(HEAD * h, HEAD * h + HEAD)
            total = out = None
            for span, score in zip(spans, scores):
                soft = jnp.exp(score - top)
                one = jnp.sum(soft, axis=0, keepdims=True)
                part = mm(vt[own, span], soft.astype(BF))
                total = one if total is None else total + one
                out = part if out is None else out + part
            mixt[own, here] = out / total
            lse[h : h + 1, here] = top + jnp.log(total)


def attend_back(kaug, qa, v, kta, qm, doa, dom, delta, lse, dk, dv, dqt, heads):
    length = kaug.shape[0]
    slope_sums = [jnp.zeros((1, BQ), F32) for _ in range(heads)]
    for i in range(length // BQ):
        off = i * BQ
        here = slice(off, off + BQ)
        turned = [None] * heads
        for span, masked in ((here, True),) + (((slice(0, off), False),) if off else ()):
            value_sum = key_sum = None
            for h in range(heads):
                soft = jnp.exp(mm(kaug[span, :], qa[h, :, here]) - lse[h : h + 1, here])
                if masked:
                    soft = jnp.where(causal(), soft, 0.0)
                score = (soft * (mm(v[span, :], doa[h, :, here]) - delta[h : h + 1, here])).astype(BF)
                one, two = mm(soft.astype(BF), dom[h, here, :]), mm(score, qm[h, here, :])
                value_sum = one if value_sum is None else value_sum + one
                key_sum = two if key_sum is None else key_sum + two
                more = mm(kta[h, :, span], score)
                turned[h] = more if turned[h] is None else turned[h] + more
            if masked:
                dv[span, :] = value_sum
                dk[span, :] = key_sum
            else:
                dv[span, :] += value_sum
                dk[span, :] += key_sum
        spot = (off + iota((1, BQ), 1)).astype(F32)
        for h in range(heads):
            dqt[HEAD * h : HEAD * h + HEAD, here] = turned[h][0:HEAD, :] * SCALE
            slope_sums[h] = slope_sums[h] + (
                turned[h][HEAD + 1 : HEAD + 2, :]
                + turned[h][HEAD + 2 : HEAD + 3, :]
                - spot * turned[h][HEAD : HEAD + 1, :]
            )
    return slope_sums


def prepare_back(q, k, do, mixt, kta, qm, doa, dom, delta, heads):
    length, width = q.shape
    kt = flip(k)
    dot = flip(do)
    lane = iota((length, width), 1)
    row = iota((width, length), 0)
    extra = iota((16, length), 0)
    column = iota((16, length), 1)
    extras = jnp.where(
        extra == 0,
        1,
        jnp.where(extra == 1, (column >> 7) << 7, jnp.where(extra == 2, column & 127, 0)),
    )
    for h in range(heads):
        own = slice(HEAD * h, HEAD * h + HEAD)
        kta[h, 0:HEAD, :] = kt[own, :].astype(BF)
        kta[h, HEAD : HEAD + 16, :] = extras.astype(F32).astype(BF)
        mine = (lane >= HEAD * h) & (lane < HEAD * h + HEAD)
        qm[h] = jnp.where(mine, q.astype(F32) * SCALE, 0.0).astype(BF)
        dom[h] = jnp.where(mine, do.astype(F32), 0.0).astype(BF)
        doa[h] = jnp.where((row >= HEAD * h) & (row < HEAD * h + HEAD), dot, 0.0).astype(BF)
        delta[h : h + 1, :] = jnp.sum(dot[own, :] * mixt[own, :], axis=0, keepdims=True)


def attend_scratch(length, width, heads, lead=()):
    wide = width + POS
    return [
        pltpu.VMEM(lead + (length, wide), BF),
        pltpu.VMEM(lead + (heads, wide, length), BF),
    ]


def back_scratch(length, width, heads):
    return [
        pltpu.VMEM((heads, HEAD + 16, length), BF),
        pltpu.VMEM((heads, length, width), BF),
        pltpu.VMEM((heads, width, length), BF),
        pltpu.VMEM((heads, length, width), BF),
        pltpu.VMEM((8, length), F32),
        pltpu.VMEM((length, width), F32),
        pltpu.VMEM((length, width), F32),
        pltpu.VMEM((width, length), F32),
    ]


NEAR = "near"
HELD = "held"
ALL = -1
LOAD = -2
FAR = "far"
PART = "part"
HOLD = "hold"
RAW = "raw"


def keeps(n):
    return n <= 4


def hold(n):
    return HOLD if keeps(n) else FAR


def held(n):
    return HELD if keeps(n) else ALL


def smem():
    return pl.BlockSpec(memory_space=pltpu.SMEM)


def vmem():
    return pl.BlockSpec(memory_space=pltpu.VMEM)


def anywhere():
    return pl.BlockSpec(memory_space=pl.ANY)


class Held:
    def __init__(self, source, target, semaphore):
        self.copy = pltpu.make_async_copy(source, target, semaphore)
        self.target = target
        self.waited = False
        self.copy.start()

    def get(self):
        if not self.waited:
            self.copy.wait()
            self.waited = True
        return self.target


class Far:
    def __init__(self, ref, out, semaphores):
        self.ref, self.out, self.semaphores = ref, out, semaphores
        self.copies = []

    def send(self, index=None):
        source = self.ref if index is None else self.ref.at[index]
        target = self.out if index is None else self.out.at[index]
        self.copies.append(pltpu.make_async_copy(source, target, self.semaphores.at[len(self.copies)]))
        self.copies[-1].start()

    def finish(self):
        if not self.copies:
            self.send()
        for copy in self.copies:
            copy.wait()


class Here:
    def __init__(self, ref):
        self.ref = ref

    def get(self):
        return self.ref

    def send(self, index=None):
        pass

    def finish(self):
        pass


def padded(shape, dtype):
    lead = 1
    for extent in shape[:-2]:
        lead *= extent
    tall = shape[-2] if len(shape) > 1 else 1
    return lead * -(-tall // 16) * 16 * -(-shape[-1] // 128) * 128 * jnp.dtype(dtype).itemsize


def in_hbm(array):
    return pltpu.with_memory_space_constraint(array, pltpu.HBM)


def in_vmem(array):
    return pltpu.with_memory_space_constraint(array, pltpu.VMEM)


def call(body, name, ins, specs, outs, scratch=(), after=(), spare=10, weight=10, aliases=None):
    held = [i for i, spec in enumerate(specs) if isinstance(spec, int)]
    shapes = [ins[i].shape[1:] if specs[i] >= 0 else ins[i].shape for i in held]
    kinds = [out[2] if len(out) > 2 else NEAR for out in outs]
    far = [i for i, kind in enumerate(kinds) if kind in (FAR, PART)]
    far_shapes = [out[0] if kind is FAR else out[0][1:] for out, kind in zip(outs, kinds)]
    more = [pltpu.VMEM(shape, ins[i].dtype) for i, shape in zip(held, shapes)]
    more += [pltpu.VMEM(far_shapes[i], outs[i][1]) for i in far]
    if held:
        more.append(pltpu.SemaphoreType.DMA((len(held),)))
    if far:
        more.append(pltpu.SemaphoreType.DMA((len(far), 8)))
    count, own = len(ins), len(scratch)
    used = sum(padded(shape, ins[i].dtype) for i, shape in zip(held, shapes))
    used += sum(padded(shape, out[1]) for shape, out, kind in zip(far_shapes, outs, kinds) if kind is not HOLD)
    used += sum(padded(a.shape, a.dtype) for a, spec in zip(ins, specs) if spec is NEAR)
    used += sum(padded(s.shape, s.dtype) for s in scratch if len(s.shape) > 1 and s.dtype in (F32, BF))
    limit = min(VMEM_LIMIT, int(used * (1.1 if spare >= 10 else 1.0)) + spare * 1024 * 1024)

    def kernel(*refs):
        refs = list(refs)
        operands = refs[:count]
        results = refs[count + len(after) : count + len(after) + len(outs)]
        rest = refs[count + len(after) + len(outs) :]
        temporary, rest = rest[:own], rest[own:]
        targets, rest = rest[: len(held)], rest[len(held) :]
        sources, rest = rest[: len(far)], rest[len(far) :]
        for at, i in enumerate(held):
            source = operands[i] if specs[i] < 0 else operands[i].at[specs[i]]
            operands[i] = Held(source, targets[at], rest[0].at[at])
        for at, i in enumerate(far):
            target = results[i].at[outs[i][3]] if kinds[i] is PART else results[i]
            results[i] = Far(sources[at], target, rest[-1].at[at])
        for i, kind in enumerate(kinds):
            results[i] = Here(results[i]) if kind is HOLD else results[i]
        for i, spec in enumerate(specs):
            operands[i] = Here(operands[i]) if spec is HELD else operands[i]
        body(*operands, *results, *temporary)
        for i in held:
            operands[i].get()
        for i in far:
            results[i].finish()

    pinned = pl.BlockSpec(memory_space=pltpu.HBM)
    spec_of = lambda spec: anywhere() if spec == LOAD else pinned if isinstance(spec, int) or spec is RAW else vmem() if spec in (NEAR, HELD) else spec
    shape_of = {NEAR: jax.ShapeDtypeStruct, HOLD: pltpu.VMEM, FAR: pltpu.HBM, PART: pltpu.HBM}
    place = lambda a, spec: in_hbm(a) if spec is RAW or isinstance(spec, int) and spec != LOAD else in_vmem(a) if spec is HELD else a
    return pl.pallas_call(
        kernel,
        out_shape=[shape_of[kind](out[0], out[1]) for out, kind in zip(outs, kinds)],
        in_specs=[spec_of(spec) for spec in specs] + [anywhere()] * len(after),
        out_specs=[pinned if kind in (FAR, PART) else vmem() for kind in kinds],
        scratch_shapes=list(scratch) + more,
        compiler_params=pltpu.CompilerParams(vmem_limit_bytes=limit),
        cost_estimate=pl.CostEstimate(flops=weight * 1000000000, bytes_accessed=0, transcendentals=0),
        name=name,
        input_output_aliases=aliases or {},
    )(*[place(a, spec) for a, spec in zip(ins, specs)], *after)


def fold(name, targets, after=(), kind=NEAR, weight=10):
    arrays = []
    for _, blocks in targets:
        for block in blocks:
            for array, _, _ in block:
                if not any(array is other for other in arrays):
                    arrays.append(array)
    where = lambda array: [i for i, other in enumerate(arrays) if other is array][0]
    outs, plan = [], []
    for dtype, blocks in targets:
        outs.append(((sum(block[0][2] for block in blocks), blocks[0][0][0].shape[-1]), dtype) + ((kind,) if kind is HOLD else ()))
        plan.append([(block[0][2], [(where(a), first) for a, first, _ in block]) for block in blocks])

    def body(*refs):
        for target, blocks in zip(refs[len(arrays) :], plan):
            target = target.ref if isinstance(target, Here) else target
            at = 0
            for count, block in blocks:
                total = sum(refs[i][first : first + count, :].astype(F32) for i, first in block)
                target[at : at + count, :] = total.astype(target.dtype)
                at += count

    return call(body, name, arrays, [NEAR] * len(arrays), outs, after=after, weight=weight)


def mask_rows(out_grad, flags, after):
    rows, d = out_grad.shape
    third = rows // 3

    def body(grad_ref, flag_ref, given, whole):
        kept = jnp.where(flag_ref[...] != 0, grad_ref[...].astype(F32), 0.0)
        for l in range(d // 128):
            whole[l] = kept[:, l * 128 : (l + 1) * 128]
        for c in range(3):
            for l in range(d // 128):
                part = slice(c * d + l * 128, c * d + (l + 1) * 128)
                given[:, part] = whole[l, pl.ds(c, third, stride=3), :].astype(BF)

    return call(
        body,
        "mask_rows",
        [out_grad, flags],
        [NEAR, NEAR],
        [((third, 3 * d), BF)],
        [pltpu.VMEM((d // 128, rows, 128), F32)],
        after=after,
    )[0]


def pass_on(array, after, weight=10):
    def body(source, target):
        target[...] = source[...]

    return call(body, "pass_on", [array], [NEAR], [(array.shape, array.dtype)], after=after, weight=weight)[0]


def load_weights(weights):
    def body(*refs):
        sources, targets, semaphores = refs[: len(weights)], refs[len(weights) : -1], refs[-1]
        loads = [
            pltpu.make_async_copy(source if layer is None else source.at[layer], target.ref, semaphores.at[i])
            for i, (source, target, (_, layer)) in enumerate(zip(sources, targets, weights))
        ]
        for load in loads:
            load.start()
        for load in loads:
            load.wait()

    return call(
        body,
        "load_weights",
        [weight for weight, _ in weights],
        [RAW] * len(weights),
        [(weight.shape[-2:], BF, HOLD) for weight, _ in weights],
        [pltpu.SemaphoreType.DMA((len(weights),))],
        weight=100,
    )


def first_rows(pieces, wq, lnp, after):
    rows, d = pieces[0].shape
    width = wq.shape[1]

    def body(*refs):
        piece_refs, (w_ref, ln_ref, attn, qkv) = refs[: len(pieces)], refs[len(pieces) :]
        for k in range(len(pieces)):
            here = slice(k * rows, (k + 1) * rows)
            norm_into(
                Rows(rows, lambda tile, k=k: piece_refs[k][tile, :].astype(F32)),
                ln_ref[0:1, :],
                ln_ref[4:5, :],
                attn,
                k * rows,
            )
            qkv[here, :] = mm(attn[here, :], w_ref.get()[...]).astype(BF)

    outs = [((len(pieces) * rows, d), BF), ((len(pieces) * rows, width), BF)]
    return call(body, "first_rows", [*pieces, wq, lnp], [NEAR] * len(pieces) + [ALL, NEAR], outs, after=after)


def first_attention(idx, slopes, pieces, early, wq, lnp, head_count, dh, after):
    n = len(pieces)
    given = [k for k in range(n) if pieces[k] is not None]
    gone = [k for k in range(n) if pieces[k] is None]
    rows, d = pieces[given[0]].shape
    width = wq.shape[1] // 3
    length = n * rows

    def body(*refs):
        idx_ref, slope_ref = refs[0], refs[1]
        piece_refs = dict(zip(given, refs[2 : 2 + len(given)]))
        early_attn, early_qkv, w_ref, ln_ref = refs[2 + len(given) : 6 + len(given)]
        refs = refs[6 + len(given) :]
        sends, refs = refs[:n], refs[n:]
        attn, qkv, mixt, lse, kaug, qa, vt, whole = refs
        s = idx_ref[0]
        place_positions(kaug, width)
        gain, bias = ln_ref[0:1, :], ln_ref[4:5, :]
        own_weights = None
        for i, k in enumerate(gone):
            at, here = rows_at((s ^ k) * rows, rows), slice(i * rows, (i + 1) * rows)
            attn.ref[at, :] = early_attn[here, :]
            qkv.ref[at, :] = early_qkv[here, :]
        for k in given:
            first = pl.multiple_of((s ^ k) * rows, TILE)
            norm_into(
                Rows(rows, lambda tile, k=k: piece_refs[k][tile, :].astype(F32)), gain, bias, attn.ref, first
            )
            if own_weights is None:
                own_weights = w_ref.get()
            at = rows_at((s ^ k) * rows, rows)
            qkv.ref[at, :] = mm(attn.ref[at, :], own_weights[...]).astype(BF)
        attn.send()
        qkv.send()
        prepare(
            qkv.ref[:, 0:width],
            qkv.ref[:, width : 2 * width],
            [slope_ref[0, s * head_count + h] for h in range(head_count)],
            kaug,
            qa,
        )
        vt[...] = flip(qkv.ref[:, 2 * width :]).astype(BF)
        if dh < width:
            mixt.ref[...] = jnp.zeros(mixt.ref.shape, F32)
        attend(kaug, qa, vt, mixt.ref, lse.ref, head_count)
        mixt.send()
        lse.send()
        whole[...] = flip(mixt.ref[...].astype(BF))
        for k in range(n):
            sends[k][...] = whole[rows_at((s ^ k) * rows, rows), 0:dh]

    outs = [((rows, dh), BF)] * n + [
        ((length, d), BF, hold(n)),
        ((length, 3 * width), BF, hold(n)),
        ((width, length), F32, hold(n)),
        ((8, length), F32, hold(n)),
    ]
    scratch = attend_scratch(length, width, head_count) + [
        pltpu.VMEM((width, length), BF),
        pltpu.VMEM((length, width), BF),
    ]
    result = call(
        body,
        "first_attention",
        [idx, slopes, *[pieces[k] for k in given], *early, wq, lnp],
        [smem(), smem()] + [NEAR] * (len(given) + 2) + [ALL, NEAR],
        outs,
        scratch,
        after=after,
    )
    return result[:n], result[n:]


CARRY = 16


def first_ffn(idx, hid, mixes, lnp, w_out, w_in, b_in, w_back, b_back, w_pool, b_pool, after):
    n = len(mixes)
    rows, d = hid.shape
    dh = mixes[0].shape[1]
    ff = b_in.shape[1]
    third = rows // 3

    def body(*refs):
        idx_ref, hid_ref = refs[0], refs[1]
        mix_refs = refs[2 : 2 + n]
        ln_ref, wo, wi, bi, wb, bb, wp, bp = refs[2 + n : 10 + n]
        full_g, pooled, mid, pack, slope, whole, owners = refs[10 + n :]
        s = idx_ref[0]
        middle = hid_ref.get()[...].astype(F32)
        wo = wo.get()
        for k in range(n):
            middle = middle + mm(mix_refs[k][...], wo[rows_at((s ^ k) * dh, dh), :])
            owners[s ^ k] = mix_refs[k][...]
        for j in range(n):
            pack.ref[0:rows, ff + d + j * dh : ff + d + (j + 1) * dh] = owners[j]
        mid.ref[...] = middle
        mid.send()
        norm_into(
            Rows(rows, lambda tile: mid.ref[tile, :]), ln_ref[1:2, :], ln_ref[5:6, :], pack.ref.at[:, ff : ff + d]
        )
        wi, wb = wi.get(), wb.get()
        ffn_forward(pack.ref.at[:, ff : ff + d], wi, bi, pack.ref, slope.ref, rows, ff)
        slope.send()
        total = mid.ref[...] + bb[0:1, :] + mm(pack.ref[0:rows, 0:ff], wb[...])
        for l in range(d // 128):
            whole[l] = total[:, l * 128 : (l + 1) * 128]
        for c in range(3):
            for l in range(d // 128):
                some = whole[l, pl.ds(c, third, stride=3), :]
                part = slice(c * d + l * 128, c * d + (l + 1) * 128)
                full_g.ref[:, part] = some
                pack.ref[rows:, part] = some.astype(BF)
        pack.send()
        wp = wp.get()
        moved = pltpu.roll(mm(pack.ref[rows:, d : 3 * d], wp[0 : 2 * d, :]), 1, 0)
        own = mm(pack.ref[rows:, 0:d], wp[2 * d :, :]) + bp[0:1, :]
        pooled[0:third, :] = (own + jnp.where(iota((third, d), 0) == 0, 0.0, moved)).astype(BF)
        pooled[third:, :] = moved[0:CARRY, :].astype(BF)

    outs = [
        ((third, 3 * d), F32, hold(n)),
        ((third + CARRY, d), BF),
        ((rows, d), F32, hold(n)),
        ((rows + third, ff + 2 * d), BF, hold(n)),
        ((rows, ff), BF, hold(n)),
    ]
    weight = HELD if keeps(n) else 0
    return call(
        body,
        "first_ffn",
        [idx, hid, *mixes, lnp, w_out, w_in, b_in, w_back, b_back, w_pool, b_pool],
        [smem(), ALL] + [NEAR] * (n + 1) + [weight, weight, NEAR, weight, NEAR, ALL, NEAR],
        outs,
        [pltpu.VMEM((d // 128, rows, 128), F32), pltpu.VMEM((n, rows, dh), BF)],
        after=after,
    )


def short_layout(n, m, d, ff):
    kw = d // n
    spans, at = {}, 0
    for name, rows, blocks in (
        ("qkv", 3 * d // m, 1),
        ("out", d // m, 1),
        ("in", kw, ff // m // kw),
        ("back", d // m, ff // n // kw),
        ("up", 3 * d // m, 1),
    ):
        spans[name] = (at, rows, blocks)
        at += rows * blocks
    return spans, at


def ffn_layout(n, m, d, ff):
    kw = d // n
    spans, at = {}, 0
    for name, rows, blocks in (
        ("out", d // m, 1),
        ("in", kw, ff // m // kw),
        ("back", d // m, ff // n // kw),
    ):
        spans[name] = (at, rows, blocks)
        at += rows * blocks
    return spans, at


def last_layout(n, m, d):
    return 3 * d // m, d // m, 3


def pool_unit(unit, n, d):
    kw = d // n
    early = unit < 2 * n
    return early, jnp.where(early, d + unit * kw, unit * kw - 2 * d)


def short_start(idx, given, w_up, w_back, layered, w_pool, after):
    n = len(given)
    third, d3 = given[0].shape
    d, ff = d3 // 3, w_back.shape[0]
    length = n * third

    def body(*refs):
        idx_ref, given_refs = refs[0], refs[1 : 1 + n]
        wu, wb = refs[1 + n].get(), refs[2 + n].get()
        sources, refs = refs[3 + n : 7 + n], refs[7 + n :]
        u, grad, branch, act_grad = refs[:4]
        targets, arrived = refs[4:8], refs[8]
        s = idx_ref[0]
        loads = []
        later = [
            pltpu.make_async_copy(source.at[1] if i < 3 else source, target.ref, arrived.at[n + i])
            for i, (source, target) in enumerate(zip(sources, targets))
        ]
        for k in range(n):
            place = u.ref.at[rows_at((s ^ k) * third, third), :]
            loads.append(pltpu.make_async_copy(given_refs[k], place, arrived.at[k]))
        for load in loads:
            load.start()
        for load in later:
            load.start()
        for load in loads:
            load.wait()
        grad.ref[...] = nt(u.ref[...], wu[...])
        branch.ref[...] = grad.ref[...].astype(BF)
        for lanes in tiles(ff, 512):
            act_grad.ref[:, lanes] = nt(branch.ref[...], wb[lanes, :]).astype(BF)
        for load in later:
            load.wait()

    outs = [
        ((length, d3), BF, HOLD),
        ((length, d), F32, HOLD),
        ((length, d), BF, HOLD),
        ((length, ff), BF, HOLD),
        *[(weight.shape[1:], BF, HOLD) for weight in layered],
        (w_pool.shape, BF, HOLD),
    ]
    return call(
        body,
        "short_start",
        [idx, *given, w_up, w_back, *layered, w_pool],
        [smem()] + [anywhere()] * n + [HELD, HELD] + [RAW] * 4,
        outs,
        [pltpu.SemaphoreType.DMA((n + 4,))],
        after=after,
        weight=100,
    )


def short_layer(
    idx, slopes, pooled, given, begun, full_g, lnp, w_qkv, w_out, w_in, b_in, w_back, b_back, w_pool, w_up, b_up, m, after
):
    n = len(pooled)
    third = pooled[0].shape[0] - CARRY
    given = [] if begun else given
    d = lnp.shape[1]
    ff = b_in.shape[1]
    rows = 3 * third
    length = n * third
    width = 128
    pairs = d // width
    kw = d // n
    spans, packed_rows = short_layout(n, m, d, ff)
    kept_pairs = pairs if length <= 512 else 1

    def body(*refs):
        idx_ref, slope_ref = refs[0], refs[1]
        pool_refs = refs[2 : 2 + n]
        given_refs, refs = refs[2 + n : 2 + n + len(given)], refs[2 + n + len(given) :]
        begun_refs, refs = refs[: len(begun)], refs[len(begun) :]
        (fg, ln_ref, wq, wo, wi, bi, wb, bb, wp, wu, bu) = refs[:11]
        block_out, full_grad, pair, keep, give, small = refs[11:17]
        (
            pooled_s, carry, attn, qkv, mixed, mixt, lse, kaug, qa, vt, middle_s, ffn_in, act, rate,
            back_s, low_grad, low, dmix, dpl, whole, into, into2, arrived,
            kta, qm, doa, dom, delta, dk, dv, dqt, *own,
        ) = refs[17:]
        if begun:
            u_all, grad_s, branch_s, act_grad = [ref.get() for ref in begun_refs]
        else:
            u_all, grad_s, branch_s = own
        s = idx_ref[0]
        mine = idx_ref[1]
        dpre, dqkv = rate, qkv
        loads = []
        for k in range(len(given)):
            place = u_all.at[rows_at((s ^ k) * third, third), :]
            loads.append(pltpu.make_async_copy(given_refs[k], place, arrived.at[k]))
            loads[-1].start()
        for k in range(n):
            pooled_s[rows_at((s ^ k) * third, third), :] = pool_refs[k][0:third, :].astype(F32)
            carry[s ^ k] = pool_refs[k][third:, :].astype(F32)
        for j in range(1, n):
            pooled_s[j * third : j * third + 1, :] += carry[j - 1, 0:1, :]
        norm_into(Rows(length, lambda tile: pooled_s[tile, :]), ln_ref[2:3, :], ln_ref[6:7, :], attn)
        wq = wq.get()
        for c in range(0, 3 * d, 256):
            qkv[:, c : c + 256] = mm(attn[...], wq[:, c : c + 256]).astype(BF)

        def again(t):
            lane = pl.multiple_of(t * width, 128)
            own = t if kept_pairs > 1 else 0
            place_positions(kaug.at[own], width)
            prepare(
                qkv[:, pl.ds(lane, width)],
                qkv[:, pl.ds(d + lane, width)],
                [slope_ref[1, 2 * t + h] for h in range(2)],
                kaug.at[own],
                qa.at[own],
            )
            return kaug.at[own], qa.at[own]

        def forward(t, _):
            lane = pl.multiple_of(t * width, 128)
            own_kaug, own_qa = again(t)
            vt[...] = flip(qkv[:, pl.ds(2 * d + lane, width)]).astype(BF)
            attend(own_kaug, own_qa, vt, mixt.at[t], lse.at[t], 2)
            mixed[:, pl.ds(lane, width)] = flip(mixt[t].astype(BF))
            return 0

        lax.fori_loop(0, pairs, forward, 0)
        wo = wo.get()
        middle_s[...] = pooled_s[...] + mm(mixed[...], wo[...])
        norm_into(Rows(length, lambda tile: middle_s[tile, :]), ln_ref[3:4, :], ln_ref[7:8, :], ffn_in)
        wi, wb = wi.get(), wb.get()
        ffn_forward(ffn_in, wi, bi, act, rate, length, ff)
        low[...] = (middle_s[...] + bb[0:1, :] + mm(act[...], wb[...])).astype(BF)
        mine_rows = rows_at(s * third, third)
        own = low[mine_rows, :]
        wu, full = wu.get(), fg.get()
        for c in range(3):
            part = slice(c * d, (c + 1) * d)
            up = mm(own, wu[:, part]) + bu[0:1, part]
            spread(whole, c, full[:, part] + up)
        for l in range(d // 128):
            block_out.ref[:, l * 128 : (l + 1) * 128] = whole[l].astype(BF)
        block_out.send()

        small = small.ref
        small[...] = jnp.zeros_like(small)
        for load in loads:
            load.wait()
        u = u_all[...]
        if not begun:
            grad_s[...] = nt(u, wu[...])
            branch_s[...] = grad_s[...].astype(BF)
        small[1:2, 0 : 3 * d] = jnp.sum(u.astype(F32), axis=0, keepdims=True)
        small[3:4, 0:d] = jnp.sum(branch_s[...].astype(F32), axis=0, keepdims=True)
        if begun:
            for lanes in tiles(ff, 512):
                value = (act_grad[:, lanes].astype(F32) * rate[:, lanes].astype(F32)).astype(BF)
                dpre[:, lanes] = value
                small[0:1, lanes] = jnp.sum(value.astype(F32), axis=0, keepdims=True)
        else:
            ffn_backward(branch_s, wb, rate, dpre, small.at[0:1, :], length, ff)
        back_s[...] = nt(dpre[...], wi[...])

        def put_middle(tile, value):
            value = grad_s[tile, :] + value
            grad_s[tile, :] = value
            low_grad[tile, :] = value.astype(BF)

        gain_late, bias_late = norm_back(
            lambda tile: middle_s[tile, :], ln_ref[3:4, :], lambda tile: back_s[tile, :], put_middle, length
        )
        dmix[...] = nt(low_grad[...], wo[...]).astype(BF)

        def backward(t, slope_row):
            lane = pl.multiple_of(t * width, 128)
            prepare_back(
                qkv[:, pl.ds(lane, width)],
                qkv[:, pl.ds(d + lane, width)],
                dmix[:, pl.ds(lane, width)],
                mixt.at[t],
                kta,
                qm,
                doa,
                dom,
                delta,
                2,
            )
            own_kaug, own_qa = (kaug.at[t], qa.at[t]) if kept_pairs > 1 else again(t)
            vt2 = qkv.at[:, pl.ds(2 * d + lane, width)]
            sums = attend_back(
                own_kaug, own_qa, vt2, kta, qm, doa, dom, delta, lse.at[t], dk, dv, dqt, 2
            )
            dqkv[:, pl.ds(lane, width)] = flip(dqt[...].astype(BF))
            dqkv[:, pl.ds(d + lane, width)] = dk[...].astype(BF)
            dqkv[:, pl.ds(2 * d + lane, width)] = dv[...].astype(BF)
            for h in range(2):
                slope_row = slope_row + lone(jnp.sum(sums[h], axis=1, keepdims=True), 2 * t + h)
            return slope_row

        slope_row = lax.fori_loop(0, pairs, backward, jnp.zeros((1, 128), F32))
        small[3:4, d : d + 128] = slope_row
        back_s[...] = nt(dqkv[...], wq[...])

        def put_pooled(tile, value):
            dpl[0, tile, :] = (grad_s[tile, :] + value).astype(BF)

        gain_early, bias_early = norm_back(
            lambda tile: pooled_s[tile, :], ln_ref[2:3, :], lambda tile: back_s[tile, :], put_pooled, length
        )
        wide = dpl[0].astype(F32)
        small[2:3, 0:d] = gain_early
        small[2:3, d : 2 * d] = gain_late
        small[2:3, 2 * d : 3 * d] = bias_early
        small[2:3, 3 * d : 4 * d] = bias_late
        small[1:2, 3 * d : 4 * d] = jnp.sum(wide, axis=0, keepdims=True)
        later = pltpu.roll(wide, length - 1, 0)
        dpl[1] = jnp.where(iota((length, d), 0) == length - 1, 0.0, later).astype(BF)
        here, after = dpl[0, mine_rows, :], dpl[1, mine_rows, :]
        pair.ref[...] = dpl[...]
        wp = wp.get()
        given_own = u_all[mine_rows, :].astype(F32)
        spread(whole, 0, given_own[:, 0:d] + nt(here, wp[2 * d :, :]))
        spread(whole, 1, given_own[:, d : 2 * d] + nt(after, wp[0:d, :]))
        spread(whole, 2, given_own[:, 2 * d :] + nt(after, wp[d : 2 * d, :]))
        for l in range(d // 128):
            full_grad.ref[:, l * 128 : (l + 1) * 128] = whole[l]
        full_grad.send()

        def put(name, block, value):
            at, count, _ = spans[name]
            at += block * count
            into[...] = flip(value.astype(BF))
            for far in range(m // 2):
                for bit, target in ((0, keep), (1, give)):
                    start = (mine ^ (2 * far + bit)) * count
                    target[far, at : at + count, :] = into[rows_at(start, count), :]

        def put_tall(name, value):
            at, count, _ = spans[name]
            into2[...] = flip(value.astype(BF))
            for far in range(m // 2):
                for bit, target in ((0, keep), (1, give)):
                    start = (mine ^ (2 * far + bit)) * count
                    target[far, at : at + count, :] = into2[rows_at(start, count), :]

        put_tall("qkv", tn(lanes_at(attn, s * kw, kw), dqkv[...]))
        put("out", 0, tn(lanes_at(mixed, s * kw, kw), low_grad[...]))
        at, count, blocks = spans["in"]
        grad_in = tn(lanes_at(ffn_in, s * kw, kw), dpre[...]).astype(BF)
        for b in range(m):
            for i in range(blocks):
                first = (b * blocks + i) * kw
                here = slice(at + i * count, at + (i + 1) * count)
                piece = grad_in[:, first : first + kw]

                def store(target, far=(mine ^ b) >> 1, here=here, piece=piece):
                    target[far, here, :] = piece

                pl.when(((mine ^ b) & 1) == 0)(lambda: store(keep))
                pl.when(((mine ^ b) & 1) == 1)(lambda: store(give))
        blocks = spans["back"][2]
        for i in range(blocks):
            put("back", i, tn(lanes_at(act, (s * blocks + i) * kw, kw), branch_s[...]))
        put_tall("up", tn(lanes_at(low, s * kw, kw), u))

    outs = [
        ((rows, d), BF, FAR),
        ((rows, d), F32, hold(n)),
        ((2, length, d), BF, hold(n)),
        ((m // 2, packed_rows, kw), BF),
        ((m // 2, packed_rows, kw), BF),
        ((8, ff), F32, hold(n)),
    ]
    scratch = [
        pltpu.VMEM((length, d), F32),
        pltpu.VMEM((n, CARRY, d), F32),
        pltpu.VMEM((length, d), BF),
        pltpu.VMEM((length, 3 * d), BF),
        pltpu.VMEM((length, d), BF),
        pltpu.VMEM((pairs, width, length), F32),
        pltpu.VMEM((pairs, 8, length), F32),
        *attend_scratch(length, width, 2, (kept_pairs,)),
        pltpu.VMEM((width, length), BF),
        pltpu.VMEM((length, d), F32),
        pltpu.VMEM((length, d), BF),
        pltpu.VMEM((length, ff), BF),
        pltpu.VMEM((length, ff), BF),
        pltpu.VMEM((length, d), F32),
        pltpu.VMEM((length, d), BF),
        pltpu.VMEM((length, d), BF),
        pltpu.VMEM((length, d), BF),
        pltpu.VMEM((2, length, d), BF),
        pltpu.VMEM((d // 128, rows, 128), F32),
        pltpu.VMEM((d, kw), BF),
        pltpu.VMEM((3 * d, kw), BF),
        pltpu.SemaphoreType.DMA((n,)),
        *back_scratch(length, width, 2),
    ]
    if not begun:
        scratch += [
            pltpu.VMEM((length, 3 * d), BF),
            pltpu.VMEM((length, d), F32),
            pltpu.VMEM((length, d), BF),
        ]
    return call(
        body,
        "short_layer",
        [idx, slopes, *pooled, *given, *begun, full_g, lnp, w_qkv, w_out, w_in, b_in, w_back, b_back, w_pool, w_up, b_up],
        [smem(), smem()]
        + [NEAR] * n
        + [anywhere()] * len(given)
        + [HELD] * len(begun)
        + [held(n), NEAR, *[HELD if begun else 1] * 3, NEAR, HELD if begun else 1, NEAR]
        + [HELD if begun else ALL] * 2
        + [NEAR],
        outs,
        scratch,
        after=after,
        spare=4 if keeps(n) else 20,
    )


def core_columns(ref, width, core):
    total = ref.shape[1]
    if width % 128 == 0:
        starts = [pl.multiple_of((2 * z + core) * width, 128) for z in range(total // width // 2)]
        return jnp.concatenate([ref[:, pl.ds(start, width)] for start in starts], axis=1)
    shape = (total, total // 2)
    row, column = iota(shape, 0), iota(shape, 1)
    block = lax.div(column, width)
    pick = row == (2 * block + core) * width + (column - block * width)
    return mm(ref[...], pick.astype(F32).astype(BF)).astype(BF)


def first_ffn_back(idx, full_grad, mid, rate, forward, lnp, w_out, w_in, w_back, fetch, n, m):
    rows, d = mid.shape
    ff = rate.shape[1]
    dh = d // n

    def body(*refs):
        idx_ref, grad_ref, mid_ref, rate_ref, forward_ref, ln_ref, wo, wi, wb = refs[:9]
        sources, refs = refs[9 : 9 + len(fetch)], refs[9 + len(fetch) :]
        sends, refs = refs[:n], refs[n:]
        middle_grad, own, give, small = refs[:4]
        targets, refs = refs[4 : 4 + len(fetch)], refs[4 + len(fetch) :]
        dpre, low_ref, branch_ref, back_s, fetched = refs
        loads = [
            pltpu.make_async_copy(source, target.ref, fetched.at[i])
            for i, (source, target) in enumerate(zip(sources, targets))
        ]
        for load in loads:
            load.start()
        s, core = idx_ref[0], idx_ref[1] & 1
        grad = grad_ref.get()[...]
        branch = grad.astype(BF)
        branch_ref[...] = branch
        sums = small.ref
        sums[...] = jnp.zeros_like(sums)
        sums[5:6, 2 * d : 3 * d] = jnp.sum(branch.astype(F32), axis=0, keepdims=True)
        wb, wi, rates = wb.get(), wi.get(), rate_ref.get()
        ffn_backward(branch_ref, wb, rates, dpre, sums.at[4:5, :], rows, ff)
        back_s[...] = nt(dpre[...], wi[...])
        middles, grads = mid_ref.get(), grad_ref.get()

        def put(tile, value):
            value = grads[tile, :] + value
            middle_grad.ref[tile, :] = value
            low_ref[tile, :] = value.astype(BF)

        gain, bias = norm_back(
            lambda tile: middles[tile, :], ln_ref[1:2, :], lambda tile: back_s[tile, :], put, rows
        )
        sums[5:6, 0:d] = gain
        sums[5:6, d : 2 * d] = bias
        small.send()
        middle_grad.send()
        wo = wo.get()
        for k in range(n):
            sends[k][0:rows, :] = nt(low_ref[...], wo[rows_at((s ^ k) * dh, dh), :]).astype(BF)
        groups = forward_ref.get().at[rows:, 0 : 3 * d]
        third = rows // 3
        for k in range(n):
            for i in range(3):
                _, start = pool_unit(3 * (s ^ k) + i, n, d)
                sends[k][rows + i * third : rows + (i + 1) * third, :] = lanes_at(groups, start, dh)
        for target, bit in ((own, 0), (give, 1)):
            target.ref[0:rows, 0 : ff // 2] = core_columns(dpre, ff // m, core ^ bit)
            target.ref[0:rows, ff // 2 : (ff + d) // 2] = core_columns(branch_ref, d // m, core ^ bit)
            target.ref[0:rows, (ff + d) // 2 :] = core_columns(low_ref, d // m, core ^ bit)
        for load in loads:
            load.wait()

    pack = (rows, ff // 2 + d)
    outs = [((2 * rows, dh), BF)] * n + [
        ((rows, d), F32, hold(n)),
        (pack, BF, hold(n)),
        (pack, BF, hold(n)),
        ((8, ff), F32, hold(n)),
        *[(array.shape, array.dtype, HOLD) for array in fetch],
    ]
    weight = HELD if keeps(n) else 0
    result = call(
        body,
        "first_ffn_back",
        [idx, full_grad, mid, rate, forward, lnp, w_out, w_in, w_back, *fetch],
        [smem()] + [held(n)] * 4 + [NEAR, weight, weight, weight] + [anywhere()] * len(fetch),
        outs,
        [pltpu.VMEM((rows, ff), BF), pltpu.VMEM((rows, d), BF), pltpu.VMEM((rows, d), BF)]
        + [pltpu.VMEM((rows, d), F32), pltpu.SemaphoreType.DMA((max(len(fetch), 1),))],
    )
    return result[:n], result[n:]


def halves(n, count):
    bits = [1 << t for t in range(n.bit_length() - 1)]
    return ((bits, range(0, count // 2)), (bits[::-1], range(count // 2, count)))


def kept_orders(n, bits):
    orders = [list(range(n))]
    for bit in bits:
        orders.append([r for r in orders[-1] if not r & bit])
    return orders


def first_ffn_weights(idx, forward, forward_other, back, back_other, n, m, d, ff, after):
    rows = forward.shape[0] // 4 * 3
    kw = d // n
    far = m // 2
    spans, packed_rows = ffn_layout(n, m, d, ff)
    plan = halves(n, far)

    def body(*refs):
        idx_ref, own_f, other_f, own_b, other_b = refs[:5]
        targets = refs[5:9]
        wide_in, wide_back, wide_out = refs[9:]
        s, mine = idx_ref[0], idx_ref[1]
        per, share, count_out = ff // m, ff // n, d // m
        f, g, b, h = own_f.get(), other_f.get(), own_b.get(), other_b.get()
        cut_in, cut_back = ff // 2, (ff + d) // 2
        turned = [flip(x[0:rows, ff : ff + d]).astype(BF) for x in (f, g)]
        for z in range(far):
            part = slice(z * per, (z + 1) * per)
            wide_in[z] = (mm(turned[0], b[0:rows, part]) + mm(turned[1], h[0:rows, part])).astype(BF)
        turned = [flip(x[0:rows, cut_in:cut_back]).astype(BF) for x in (b, h)]
        for j in range(n):
            part = slice(j * share, (j + 1) * share)
            wide_back[j] = (mm(turned[0], f[0:rows, part]) + mm(turned[1], g[0:rows, part])).astype(BF)
        turned = [flip(x[0:rows, cut_back:]).astype(BF) for x in (b, h)]
        for j in range(n):
            part = slice(ff + d + j * kw, ff + d + (j + 1) * kw)
            wide_out[j] = (mm(turned[0], f[0:rows, part]) + mm(turned[1], g[0:rows, part])).astype(BF)
        for half, (bits, places) in enumerate(plan):
            order = kept_orders(n, bits)[0]
            keeps_, gives = [r for r in order if not r & bits[0]], [r for r in order if r & bits[0]]
            for target, chosen in ((targets[2 * half], keeps_), (targets[2 * half + 1], gives)):
                first = 0
                for r in chosen:
                    j = s ^ r
                    for zr in places:
                        z = (mine >> 1) ^ zr
                        at, count, _ = spans["out"]
                        target[first + at : first + at + count, :] = wide_out[j, rows_at(z * count, count), :]
                        at, count, blocks = spans["in"]
                        for i in range(blocks):
                            target[first + at + i * count : first + at + (i + 1) * count, :] = wide_in[
                                z, rows_at(j * kw, kw), i * kw : (i + 1) * kw
                            ]
                        at, count, blocks = spans["back"]
                        for i in range(blocks):
                            target[first + at + i * count : first + at + (i + 1) * count, :] = wide_back[
                                j, rows_at(z * count, count), i * kw : (i + 1) * kw
                            ]
                        first += packed_rows

    outs = [((n // 2 * (far // 2) * packed_rows, kw), BF)] * 4
    scratch = [
        pltpu.VMEM((far, d, ff // m), BF),
        pltpu.VMEM((n, d // 2, ff // n), BF),
        pltpu.VMEM((n, d // 2, kw), BF),
    ]
    return call(
        body,
        "first_ffn_weights",
        [idx, forward, forward_other, back, back_other],
        [smem(), held(n), HELD if keeps(n) else LOAD, held(n), HELD if keeps(n) else LOAD],
        outs,
        scratch,
        after=after,
    )


SMALL = 16


def small_layout(m, kw, d, ff):
    places, row = {}, 0
    for name, size in (("in0", ff // m), ("in1", ff // m), ("up", 3 * d // m)):
        places[name] = (row, 0, size)
        row += -(-size // kw)
    for one, two in (
        ("gain00", "gain01"),
        ("gain10", "gain11"),
        ("bias00", "bias01"),
        ("bias10", "bias11"),
        ("back0", "back1"),
        ("pool", None),
    ):
        places[one] = (row, 0, d // m)
        if two:
            places[two] = (row, kw // 2, d // m)
        row += 1
    places["slopes"] = (row, 0, 0)
    return places


def first_attention_back(
    idx, slopes, qkv, attn, mixt, lse, grads, wq, lnp, small_short, small_ffn, pooled_grad, head_count, dh, m, after
):
    n = len(grads)
    length, d = attn.shape
    rows = length // n
    third = rows // 3
    width = wq.shape[1] // 3
    kw = d // n
    ff = small_ffn.shape[1]
    heads = slopes.shape[1]

    def body(*refs):
        idx_ref, slope_ref, qkv_ref, attn_ref, mixt_ref, lse_ref = refs[:6]
        grad_refs = refs[6 : 6 + n]
        w_ref, ln_ref, short_ref, ffn_ref, pooled_ref = refs[6 + n : 11 + n]
        refs = refs[11 + n :]
        shares, sends, pool = refs[:n], refs[n : 2 * n], refs[2 * n]
        kaug, qa, do, turned, owners, table, groups, kta, qm, doa, dom, delta, dk, dv, dqt = refs[2 * n + 1 :]
        s = idx_ref[0]
        if dh < width:
            do[...] = jnp.zeros_like(do)
            dqt[...] = jnp.zeros_like(dqt)
        for k in range(n):
            do[rows_at((s ^ k) * rows, rows), 0:dh] = grad_refs[k][0:rows, :]
            for i in range(3):
                here = slice(rows + i * third, rows + (i + 1) * third)
                groups[i, rows_at((s ^ k) * third, third), :] = grad_refs[k][here, :]
        place_positions(kaug, width)
        qkv_ref = qkv_ref.get()
        q, k_ = qkv_ref[:, 0:width], qkv_ref[:, width : 2 * width]
        prepare(q, k_, [slope_ref[0, s * head_count + h] for h in range(head_count)], kaug, qa)
        prepare_back(q, k_, do[...], mixt_ref.get(), kta, qm, doa, dom, delta, head_count)
        sums = attend_back(
            kaug, qa, qkv_ref.at[:, 2 * width :], kta, qm, doa, dom, delta, lse_ref.get(), dk, dv, dqt, head_count
        )
        turned[0:width, :] = dqt[...].astype(BF)
        turned[width : 2 * width, :] = flip(dk[...].astype(BF))
        turned[2 * width :, :] = flip(dv[...].astype(BF))
        do[...] = flip(dqt[...].astype(BF))
        for k in range(n):
            here = rows_at((s ^ k) * rows, rows)
            sends[k][0:rows, :] = do[here, 0:dh]
            sends[k][rows : 2 * rows, :] = dk[here, 0:dh].astype(BF)
            sends[k][2 * rows : 3 * rows, :] = dv[here, 0:dh].astype(BF)
        grad_w = mm(turned[...], attn_ref.get()[...])
        for j in range(n):
            for g in range(3):
                owners[j, g * dh : (g + 1) * dh, :] = grad_w[
                    g * width : g * width + dh, j * kw : (j + 1) * kw
                ].astype(BF)
        w_turned = flip(w_ref.get()[...]).astype(F32)
        gain, bias = ln_ref[0:1, :], ln_ref[4:5, :]
        column = jnp.sum(turned[...].astype(F32), axis=1, keepdims=True)
        bias_grad = jnp.sum(w_turned * column, axis=0, keepdims=True)
        gain_grad = (jnp.sum(w_turned * grad_w, axis=0, keepdims=True) - bias * bias_grad) / gain
        once = jnp.where(s == 0, 1.0, 0.0)
        both = ffn_ref.get()[...] + once * short_ref.get()[...]
        slope_row = jnp.zeros((1, 128), F32)
        for h in range(head_count):
            slope_row = slope_row + lone(jnp.sum(sums[h], axis=1, keepdims=True), s * head_count + h)
        table[...] = jnp.zeros_like(table)
        vectors = {
            "in0": both[4:5, :],
            "in1": both[0:1, :],
            "up": both[1:2, 0 : 3 * d],
            "gain00": gain_grad,
            "gain01": both[5:6, 0:d],
            "gain10": both[2:3, 0:d],
            "gain11": both[2:3, d : 2 * d],
            "bias00": bias_grad,
            "bias01": both[5:6, d : 2 * d],
            "bias10": both[2:3, 2 * d : 3 * d],
            "bias11": both[2:3, 3 * d : 4 * d],
            "back0": both[5:6, 2 * d : 3 * d],
            "back1": both[3:4, 0:d],
            "pool": both[1:2, 3 * d : 4 * d],
        }
        for name, (row, lane, size) in small_layout(m, kw, d, ff).items():
            for b in range(m):
                if name == "slopes":
                    table[b * SMALL + row : b * SMALL + row + 1, 0:heads] = slope_row[:, 0:heads]
                    table[b * SMALL + row : b * SMALL + row + 1, heads : 2 * heads] = both[3:4, d : d + heads]
                    continue
                for at in range(0, size, kw):
                    span = min(kw, size - at)
                    spot = b * SMALL + row + at // kw
                    first = b * size + at
                    table[spot : spot + 1, lane : lane + span] = vectors[name][:, first : first + span]
        pooled_ref = pooled_ref.get()
        for i in range(3):
            early, _ = pool_unit(3 * s + i, n, d)
            pool[i * d : (i + 1) * d, :] = flip(tn(groups[i], pooled_ref[early.astype(jnp.int32)]).astype(BF))
        for k in range(n):
            shares[k][0 : 3 * dh, :] = owners[s ^ k]
            shares[k][3 * dh :, :] = table[...].astype(BF)

    outs = [((3 * dh + m * SMALL, kw), BF)] * n + [((3 * rows, dh), BF)] * n + [((3 * d, kw), BF)]
    scratch = (
        attend_scratch(length, width, head_count)
        + [
            pltpu.VMEM((length, width), BF),
            pltpu.VMEM((3 * width, length), BF),
            pltpu.VMEM((n, 3 * dh, kw), BF),
            pltpu.VMEM((m * SMALL, kw), F32),
            pltpu.VMEM((3, n * third, kw), BF),
        ]
        + back_scratch(length, width, head_count)
    )
    result = call(
        body,
        "first_attention_back",
        [idx, slopes, qkv, attn, mixt, lse, *grads, wq, lnp, small_short, small_ffn, pooled_grad],
        [smem(), smem()] + [held(n)] * 4 + [NEAR] * n + [ALL, NEAR, held(n), held(n), held(n)],
        outs,
        scratch,
        after=after,
    )
    return result[:n], result[n : 2 * n], result[2 * n]


def input_gradient(idx, pieces, w_qkv, hid, middle_grad, lnp, after):
    n = len(pieces)
    dh = pieces[0].shape[1]
    rows, d = hid.shape

    def body(*refs):
        idx_ref = refs[0]
        piece_refs = refs[1 : 1 + n]
        w_ref, hid_ref, mid_ref, ln_ref, out, owners, whole, back = refs[1 + n :]
        s = idx_ref[0]
        for k in range(n):
            owners[s ^ k] = piece_refs[k][0 : 3 * rows, :]
        for j in range(n):
            for g in range(3):
                whole[:, g * d + j * dh : g * d + (j + 1) * dh] = owners[j, g * rows : (g + 1) * rows, :]
        back[...] = nt(whole[...], w_ref.get()[...])
        hid_ref, mid_ref = hid_ref.get(), mid_ref.get()

        def put(tile, value):
            out.ref[tile, :] = mid_ref[tile, :] + value

        norm_back(
            lambda tile: hid_ref[tile, :].astype(F32), ln_ref[0:1, :], lambda tile: back[tile, :], put, rows
        )

    scratch = [pltpu.VMEM((n, 3 * rows, dh), BF), pltpu.VMEM((rows, 3 * d), BF), pltpu.VMEM((rows, d), F32)]
    return call(
        body,
        "input_gradient",
        [idx, *pieces, w_qkv, hid, middle_grad, lnp],
        [smem()] + [NEAR] * n + [0, ALL, held(n), NEAR],
        [((rows, d), F32, FAR)],
        scratch,
        after=after,
        weight=0,
    )[0]


def order_shares(idx, pieces, pool, m, d, after):
    n = len(pieces)
    kw = pieces[0].shape[1]
    per, block, blocks = last_layout(n, m, d)
    every = per + block * blocks + SMALL
    dh = kw

    def body(*refs):
        idx_ref = refs[0]
        piece_refs = refs[1 : 1 + n]
        pool_ref, keep, give_near, give_far, natural, table = refs[1 + n :]
        s, mine = idx_ref[0], idx_ref[1]
        total = jnp.zeros((m * SMALL, kw), F32)
        for k in range(n):
            for g in range(3):
                at = g * dh
                natural[rows_at(g * d + (s ^ k) * dh, dh), :] = piece_refs[k][at : at + dh, :]
            total = total + piece_refs[k][3 * dh :, :].astype(F32)
        table[...] = total.astype(BF)
        for rel in range(m):
            target = (give_far if rel >= m // 2 else give_near) if rel & 1 else keep
            at = ((rel >> 1) % (m // 4) if rel & 1 else rel >> 1) * every
            b = mine ^ rel
            target[at : at + per, :] = natural[rows_at(b * per, per), :]
            for i in range(blocks):
                here = slice(at + per + i * block, at + per + (i + 1) * block)
                target[here, :] = pool_ref[rows_at(i * d + b * block, block), :]
            target[at + every - SMALL : at + every, :] = table[rows_at(b * SMALL, SMALL), :]

    return call(
        body,
        "order_shares",
        [idx, *pieces, pool],
        [smem()] + [NEAR] * (n + 1),
        [((m // 2 * every, kw), BF)] + [((m // 4 * every, kw), BF)] * 2,
        [pltpu.VMEM((3 * d, kw), BF), pltpu.VMEM((m * SMALL, kw), BF)],
        after=after,
    )


def unpack(held, spans, which, kw, n, qkv, out, inner, back):
    for j in range(n):
        lanes = slice(j * kw, (j + 1) * kw)
        for name, target in (("qkv", qkv), ("out", out)):
            at, count, _ = spans[name]
            target[:, lanes] = held[j, at : at + count, :].astype(F32)
        at, count, blocks = spans["in"]
        for i in range(blocks):
            inner[lanes, i * kw : (i + 1) * kw] = held[j, at + i * count : at + (i + 1) * count, :].astype(F32)
        at, count, blocks = spans["back"]
        for i in range(blocks):
            first = (j * blocks + i) * kw
            back[:, first : first + kw] = held[j, at + i * count : at + (i + 1) * count, :].astype(F32)


def both_layers(n, m, d, ff, which):
    shapes = ((2, 3 * d // m, d), (2, d // m, d), (2, d, ff // m), (2, d // m, ff))
    return [(shape, F32, PART, which) for shape in shapes]


def finish_short(idx, parts, skip, small, n, m, d, ff, heads, after):
    kw = d // n
    spans, _ = short_layout(n, m, d, ff)

    def body(*refs):
        idx_ref, part_refs, small = refs[0], refs[1 : 1 + n], refs[1 + n]
        qkv, out, inner, back, up = refs[2 + n : 7 + n]
        gains, biases, slopes, in_bias, back_bias, pool_bias, up_bias, held = refs[7 + n :]
        s = idx_ref[0]
        for k in range(n):
            held[s ^ k] = part_refs[k][skip if k else 0 :, :]
        unpack(held, spans, 1, kw, n, qkv.ref, out.ref, inner.ref, back.ref)
        for target in (qkv, out, inner, back):
            target.send()
        for j in range(n):
            at, count, _ = spans["up"]
            up.ref[:, j * kw : (j + 1) * kw] = held[j, at : at + count, :].astype(F32)
        up.send()
        places = small_layout(m, kw, d, ff)

        def pick(name, count):
            row, lane, _ = places[name]
            return small[row : row + 1, lane : lane + count]

        for which in range(2):
            for norm_at in range(2):
                name = str(which) + str(norm_at)
                gains[which, norm_at : norm_at + 1, :] = pick("gain" + name, d // m)
                biases[which, norm_at : norm_at + 1, :] = pick("bias" + name, d // m)
            back_bias[which : which + 1, :] = pick("back" + str(which), d // m)
            row = places["slopes"][0]
            slopes[which : which + 1, :] = small[row : row + 1, which * heads : (which + 1) * heads]
        pool_bias[...] = pick("pool", d // m)
        for at in range(0, ff // m, kw):
            for which in range(2):
                row = places["in" + str(which)][0] + at // kw
                in_bias[which : which + 1, at : at + kw] = small[row : row + 1, :]
        for at in range(0, 3 * d // m, kw):
            span = min(kw, 3 * d // m - at)
            row = places["up"][0] + at // kw
            up_bias[:, at : at + span] = small[row : row + 1, 0:span]

    outs = both_layers(n, m, d, ff, 1) + [
        ((3 * d // m, d), F32, FAR),
        ((2, 2, d // m), F32),
        ((2, 2, d // m), F32),
        ((2, heads), F32),
        ((2, ff // m), F32),
        ((2, d // m), F32),
        ((1, d // m), F32),
        ((1, 3 * d // m), F32),
    ]
    return call(
        body,
        "finish_short",
        [idx, *parts, small],
        [smem()] + [NEAR] * (n + 1),
        outs,
        [pltpu.VMEM((n,) + parts[0].shape, BF)],
        after=after,
        weight=0,
    )


def finish_first(idx, parts, begun, n, m, d, ff):
    kw = d // n
    spans, rows = ffn_layout(n, m, d, ff)
    per, block, blocks = last_layout(n, m, d)
    spans = dict(spans, qkv=(rows, per, 1), pool=(rows + per, block, blocks))

    def body(*refs):
        idx_ref, part_refs = refs[0], refs[1 : 1 + n]
        qkv, out, inner, back, pool, held = refs[5 + n :]
        s = idx_ref[0]
        for k in range(n):
            held[s ^ k] = part_refs[k][...]
        unpack(held, spans, 0, kw, n, qkv.ref, out.ref, inner.ref, back.ref)
        for target in (qkv, out, inner, back):
            target.send()
        for j in range(n):
            at, count, blocks = spans["pool"]
            for i in range(blocks):
                first = (j * blocks + i) * kw
                pool.ref[:, first : first + kw] = held[j, at + i * count : at + (i + 1) * count, :].astype(F32)
        pool.send()

    outs = both_layers(n, m, d, ff, 0) + [((d // m, 3 * d), F32, FAR)]
    return call(
        body,
        "finish_first",
        [idx, *parts, *begun],
        [smem()] + [NEAR] * n + [RAW] * 4,
        outs,
        [pltpu.VMEM((n,) + parts[0].shape, BF)],
        aliases={n + 1 + i: i for i in range(4)},
    )


def swap(array, axis, by):
    count = lax.axis_size(axis)
    return lax.ppermute(array, axis, [(i, i ^ by) for i in range(count)])


def gather(array, axis):
    return [array] + [swap(array, axis, k) for k in range(1, lax.axis_size(axis))]


def exchange(arrays, axis):
    return [arrays[0]] + [swap(arrays[k], axis, k) for k in range(1, len(arrays))]


def local(
    hidden_in, out_grad, start_flags, ln_gain, ln_bias, w_qkv, w_out, slopes, w_in, b_in, w_back, b_back,
    w_pool, b_pool, w_up, b_up,
):
    n, m = lax.axis_size("seq"), lax.axis_size("batch")
    s, mine = lax.axis_index("seq"), lax.axis_index("batch")
    idx = jnp.stack([s, mine]).astype(jnp.int32)
    hid = hidden_in[0]
    rows, d = hid.shape
    ff = w_in.shape[2]
    heads = slopes.shape[1]
    head_count = heads // n
    dh = head_count * HEAD
    width = max(dh, 128)
    far = m // 2
    row = lambda v: v.astype(F32).reshape(1, -1)

    hidden_parts = gather(hid, "seq")
    lnp = jnp.concatenate([ln_gain.reshape(4, d), ln_bias.reshape(4, d)], axis=0).astype(F32)
    columns = [lax.dynamic_slice(w_qkv, (0, 0, g * d + s * dh), (1, d, dh))[0] for g in range(3)]
    wq = jnp.concatenate([jnp.pad(c, ((0, 0), (0, width - dh))) for c in columns], axis=1)
    loaded = [w_out, w_in, w_back]
    up_held, back_held = w_up, w_back
    if keeps(n):
        *loaded, up_held, back_held = load_weights([(w_out, 0), (w_in, 0), (w_back, 0), (w_up, None), (w_back, 1)])
    early = first_rows([hid, hidden_parts[n - 1]], wq, lnp, loaded[:1])
    given = mask_rows(out_grad[0], start_flags[0][:, None], [*hidden_parts[1:], early[1]])
    given_parts = [swap(given, "seq", k) for k in range(1, n - 1)]

    sends, (attn, qkv, mixt, lse) = first_attention(
        idx, slopes, [None, *hidden_parts[1 : n - 1], None], early, wq, lnp, head_count, dh, [given]
    )
    mixes = exchange(sends, "seq")
    given = pass_on(given, [*mixes[1:], *given_parts])
    last_given = swap(given, "seq", n - 1)
    full_g, pooled, mid, forward, rate = first_ffn(
        idx, hid, mixes, lnp, loaded[0], loaded[1], row(b_in[0]), loaded[2], row(b_back[0]), w_pool, row(b_pool),
        [given],
    )
    pooled_parts = gather(pooled, "seq")
    forward_other = swap(forward, "batch", 1)
    given_parts = [given] + given_parts + [last_given]
    begun, short_weights = [], [w_qkv, w_out, w_in, w_pool]
    if keeps(n):
        result = short_start(idx, given_parts, up_held, back_held, short_weights[:3], w_pool, [mid])
        begun, short_weights = result[:4], result[4:]
    block_out, full_grad, pair, keep, give, small_short = short_layer(
        idx, slopes, pooled_parts, given_parts, begun, full_g, lnp, *short_weights[:3], row(b_in[1]), back_held,
        row(b_back[1]), short_weights[3], up_held, row(b_up), m, [],
    )

    short_rows = keep.shape[1]
    keep, give = keep.reshape(-1, keep.shape[2]), give.reshape(-1, keep.shape[2])
    other = swap(give, "batch", 1)
    sends, (middle_grad, back, give, small_ffn, *fetched) = first_ffn_back(
        idx, full_grad, mid, rate, forward, lnp, *loaded, [forward_other] if keeps(n) else [], n, m
    )
    forward_other = fetched[0] if fetched else forward_other
    back_other = swap(give, "batch", 1)
    grads = exchange(sends, "seq")

    def split(parts, count, size, places):
        return [
            (BF, [[(part, i * size, size) for part in parts] for i in range(count) if places(i)]),
            (BF, [[(part, i * size, size) for part in parts] for i in range(count) if not places(i)]),
        ]

    even = lambda i: i % 2 == 0
    packs = first_ffn_weights(idx, forward, forward_other, back, back_other, n, m, d, ff, [])
    short_keep, short_give = fold("short_chip", split([keep, other], far, short_rows, even), [packs[0]])
    short_other = swap(short_give, "batch", 2)
    plan = halves(n, far)
    others = [swap(packs[2 * half + 1], "seq", bits[0]) for half, (bits, _) in enumerate(plan)]
    packs = [packs[0], packs[2]]
    shares, sends, pool = first_attention_back(
        idx, slopes, qkv, attn, mixt, lse, grads, wq, lnp, small_short, small_ffn, pair, head_count, dh, m, [short_keep]
    )
    shares = exchange(shares, "seq")

    size = ffn_layout(n, m, d, ff)[1]
    steps = n.bit_length() - 1
    short_count, after = far // 2, [shares[0]]
    for step in range(1, steps):
        targets, rest = [], []
        for (bits, places), pack, other in zip(plan, packs, others):
            orders = kept_orders(n, bits)[step]
            per = len(places) * size
            keeping = [i for i, r in enumerate(orders) if not r & bits[step]]
            targets += split([pack, other], len(orders), per, lambda i: i in keeping)
        if short_count > 1:
            targets += split([short_keep, short_other], short_count, short_rows, even)
        result = fold("first_plane", targets, after)
        packs, others = [result[0], result[2]], [result[1], result[3]]
        others = [swap(other, "seq", bits[step]) for (bits, _), other in zip(plan, others)]
        if short_count > 1:
            short_keep, short_other = result[4], swap(result[5], "batch", 2 * far // short_count)
            short_count //= 2
        after = [result[0]]
    while short_count > 1:
        short_keep, short_give = fold("short_plane", split([short_keep, short_other], short_count, short_rows, even))
        short_other = swap(short_give, "batch", 2 * far // short_count)
        short_count //= 2

    keep, *gives = order_shares(idx, shares, pool, m, d, after)
    last_rows = keep.shape[0] // far
    last_other = [swap(give, "batch", 1) for give in gives]
    short_sum = [(short_keep, 0, short_rows), (short_other, 0, short_rows)]

    def plane(z):
        half = z // (far // 2)
        at = (z - half * (far // 2)) * size
        return [(packs[half], at, size), (others[half], at, size)]

    def pieces(z):
        return [plane(z), [(keep, z * last_rows, last_rows), (last_other[2 * z // far], z % (far // 2) * last_rows, last_rows)]]

    result_keep, result_give = fold(
        "last_near",
        [(BF, [block for z in range(far) if z % 2 == odd for block in pieces(z)]) for odd in range(2)],
        [keep],
        weight=0,
    )
    short_total, *messages = fold(
        "short_total",
        [(BF, [short_sum])] + [(BF, [[(sends[k], 0, sends[k].shape[0])], short_sum]) for k in range(1, n)],
        [result_keep],
        weight=100,
    )
    both, count = size + last_rows, far // 2
    other = swap(result_give, "batch", 2)
    messages = [swap(message, "seq", k + 1) for k, message in enumerate(messages)]
    after = [short_total]
    while count > 1:
        blocks = [[(part, i * both, both) for part in (result_keep, other)] for i in range(count)]
        result_keep, result_give = fold(
            "last_plane",
            [(BF, [blocks[i] for i in range(count) if i % 2 == odd]) for odd in range(2)],
            after,
            weight=0,
        )
        other = swap(result_give, "batch", 2 * far // count)
        count //= 2
    count = both - SMALL
    parts = [result_keep, other]
    first_total, smalls = fold(
        "first_total",
        [(BF, [[(part, 0, count) for part in parts]]), (F32, [[(part, count, SMALL) for part in parts]])],
        weight=0,
    )
    first_parts = gather(first_total, "seq")
    hidden_grad = input_gradient(idx, [sends[0], *messages], w_qkv, hid, middle_grad, lnp, [first_total])
    short_parts = [short_total, *messages]
    *begun, g_up, gains, biases, slope_grad, in_bias, back_bias, pool_bias, up_bias = finish_short(
        idx, short_parts, sends[0].shape[0], smalls, n, m, d, ff, heads, [in_hbm(hidden_grad)]
    )
    g_qkv, g_out, g_in, g_back, g_pool = finish_first(idx, first_parts, begun, n, m, d, ff)
    turn = lambda a: jnp.swapaxes(a, -1, -2)
    return (
        block_out[None],
        hidden_grad[None],
        gains,
        biases,
        turn(g_qkv),
        turn(g_out),
        slope_grad,
        g_in,
        in_bias,
        turn(g_back),
        back_bias,
        turn(g_pool),
        pool_bias[0],
        turn(g_up),
        up_bias[0],
    )


def solution(mesh):
    rows = P("batch", "seq", None)
    last = P(None, None, "batch")
    in_specs = (rows, rows, P("batch", "seq")) + (P(),) * 13
    out_specs = (
        rows,
        rows,
        last,
        last,
        last,
        last,
        P(),
        last,
        P(None, "batch"),
        last,
        P(None, "batch"),
        P(None, "batch"),
        P("batch"),
        P(None, "batch"),
        P("batch"),
    )
    return jax.shard_map(local, mesh=mesh, in_specs=in_specs, out_specs=out_specs, check_vma=False)
```
